256 devices in a mesh: proto: 64 (over z, x, core), view: 4 (over y).
Axes of the slice: x: 4, y: 4, z: 8, core: 2. Of those that a mesh axis runs over, the one named last changes fastest.
Arguments:
- features: float32 [6144, 2, 256], P(('view', 'proto')), may hold values from -6 to 6
- prototypes: float32 [65536, 256], P('proto'), may hold values from -6 to 6
- code_counts: int32 [6144, 2, 65536], P('view', None, 'proto'), may hold values from 0 to 1023
Outputs:
- features_grad: float32 [6144, 2, 256], P(('view', 'proto'))
- proto_grad: float32 [65536, 256], P('proto')
The draws below stay inside these ranges and needn't reach their ends.
All inputs are finite; a program needn't handle non-finite values.
Results may differ from the reference program's by a relative error of at most 0.0003.
Values sent between devices are 32-bit elements; how exact they have to be, the bound alone decides.
A program may use at most 128 MiB of HBM per device.

```python
import math
import jax
import jax.numpy as jnp
import numpy as np
from jax import lax

D = 256
CROPS = 2
PROTOS = 65536
VIEWS = 6144


def place_ends(array, key, smallest, high):
    spot = [jax.random.randint(jax.random.fold_in(key, axis), (), 0, length) for axis, length in enumerate(array.shape)]
    longest = array.shape.index(max(array.shape))
    next_to = spot[:longest] + [(spot[longest] + 1) % array.shape[longest]] + spot[longest + 1:]
    return array.at[tuple(spot)].set(smallest).at[tuple(next_to)].set(high)


def steps_of(own_key, shape, split, least, high):
    level, own = 1.0, jax.random.fold_in(own_key, 6)
    for axis_at, parts in split:
        draws = jnp.exp(jax.random.uniform(jax.random.fold_in(own, axis_at), (parts,), jnp.float32, least / len(split), high / len(split)))
        level = level * jnp.repeat(draws, shape[axis_at] // parts).reshape([-1 if axis == axis_at else 1 for axis in range(len(shape))])
    return level


def rank_table(count, slope):
    weights = [(1 << 20) // math.isqrt(standing ** slope) + 1 for standing in range(1, count + 1)]
    scale = 1 + sum(weights) // (1 << 30)
    return np.cumsum(np.array([max(1, weight // scale) for weight in weights]))


def ranked(rng, extent, count, slope):
    listing = rank_table(count, slope)
    pick = jax.random.randint(jax.random.fold_in(rng, 1), extent, 0, int(listing[count - 1]))
    standing = jnp.searchsorted(jnp.asarray(listing, jnp.int32), pick, side="right")
    return jax.random.permutation(jax.random.fold_in(rng, 2), count)[standing].astype(jnp.int32)


def noise(own_key, dims, deviation, reach, split=(), kind=jnp.bfloat16):
    result = deviation * jax.random.normal(own_key, dims, jnp.float32)
    if split:
        result = result * steps_of(own_key, dims, split, -0.22, 0.18)
    return jnp.clip(result, -reach, reach).astype(kind)


def setup_inputs(seed: int = 0) -> dict:
    streams_of = jax.random.split(jax.random.key(seed), 4)
    return {
        "features": noise(streams_of[0], (VIEWS, CROPS, D), 1.0, 6.0, ((0, 256),), jnp.float32),
        "prototypes": noise(streams_of[1], (PROTOS, D), 1.0, 6.0, ((0, 64),), jnp.float32),
        "code_counts": place_ends(ranked(streams_of[2], (VIEWS, CROPS, PROTOS), 1024, 2), jax.random.fold_in(streams_of[2], 3), 0, 1023).astype(jnp.int32),
    }


SOFTMAX_TEMP = 0.1
SCALE_OF_LOSS = 4096.0
FIXED_POINT = 2.0 ** (-24)

def block_gradient(normed_rows, count_rows, cluster_center):
    largest_logit = lax.Precision.HIGHEST
    score_matrix = jnp.einsum('vhf,xf->vhx', normed_rows, cluster_center, precision=largest_logit) / SOFTMAX_TEMP
    exponent = jnp.exp(score_matrix)
    totals = lax.optimization_barrier(jnp.sum(exponent, axis=2))
    swapped = count_rows[:, ::-1, :].astype(jnp.float32) * FIXED_POINT
    masses = lax.optimization_barrier(jnp.sum(swapped, axis=2))
    weight_factor = SCALE_OF_LOSS / SOFTMAX_TEMP
    gradient = weight_factor * ((masses / totals)[:, :, None] * exponent - swapped)
    unit_grad = jnp.einsum('bjk,kd->bjd', gradient, cluster_center, precision=largest_logit)
    partial_grad = jnp.einsum('bjk,bjd->kd', gradient, normed_rows, precision=largest_logit)
    return (unit_grad, partial_grad)

def reference(features, prototypes, code_counts):
    proto_norm = jnp.sqrt(lax.optimization_barrier(jnp.sum(prototypes * prototypes, axis=1, keepdims=True)) + 1e-06)
    cluster_center = prototypes / proto_norm
    feature_norm = jnp.sqrt(lax.optimization_barrier(jnp.sum(features * features, axis=2, keepdims=True)) + 1e-06)
    unit = features / feature_norm
    block_size = math.gcd(VIEWS, 256)
    blocks = VIEWS // block_size

    def step(summed, position):
        first = position * block_size
        normed_rows = lax.dynamic_slice_in_dim(unit, first, block_size, 0)
        count_rows = lax.dynamic_slice_in_dim(code_counts, first, block_size, 0)
        unit_grad, partial_grad = block_gradient(normed_rows, count_rows, cluster_center)
        return (summed + partial_grad, unit_grad)
    initial = jnp.zeros((PROTOS, D), jnp.float32)
    proto_grad, unit_grads = lax.scan(step, initial, jnp.arange(blocks, dtype=jnp.int32))
    unit_grad = unit_grads.reshape((VIEWS, CROPS, D))
    inner_product = lax.optimization_barrier(jnp.sum(unit * unit_grad, axis=2, keepdims=True))
    features_grad = (unit_grad - unit * inner_product) / feature_norm
    return (features_grad, proto_grad)
```

```python
import jax
import jax.numpy as jnp
from jax import lax
from jax.experimental import pallas as pl
from jax.experimental.pallas import tpu as pltpu
from jax.sharding import PartitionSpec as P

MESH = pl.DeviceIdType.MESH
F32 = jnp.float32
BF16 = jnp.bfloat16
WEIGHT = 4096.0 / 0.1
FIXED_POINT = 2.0 ** (-24)
SCORE_SCALE = 10.0 * 1.4426950408889634

D = 256
KL = 1024
BLK = 48
CH = 4 * BLK
NC = 16
ROWS = NC * CH
ZN, XN = 8, 4

ORDER = [
    ("A", 0), ("A", -1),
    ("A", 1), ("A", 2),
    ("A", -2), ("B", 0, 0),
    ("B", 0, 1), ("A", 3),
    ("A", -3), ("B", -1, 0),
    ("B", 1, 1), ("A", 4),
    ("B", -1, 1), ("B", 1, 0),
    ("B", 2, 0), ("B", 2, 1),
]
POS = {name: at for at, name in enumerate(ORDER)}
BACK = [
    ("B", 2, 0), ("B", 2, 1),
    ("A", 4), ("A", -3),
    ("A", 3), ("B", -1, 0),
    ("B", 1, 1), ("B", -1, 1),
    ("B", 1, 0), ("A", -2),
    ("A", 2), ("A", -1),
    ("A", 1), ("B", 0, 0),
    ("B", 0, 1), ("A", 0),
]
SIB = {}
for _kind in "AB":
    for _at, _name in enumerate([n for n in BACK if n[0] == _kind]):
        SIB[_name] = _at

_NAMES = (
    ["cnt", "pro", "x0", "x1", "x2", "a0"]
    + ["al%d" % t for t in range(1, 5)] + ["ar%d" % t for t in range(1, 5)]
    + ["bl%d" % t for t in range(1, 5)] + ["br%d" % t for t in range(1, 5)]
    + ["b%d" % t for t in range(8)]
    + ["s%d" % t for t in range(8)]
    + ["L%d" % t for t in range(4)] + ["R%d" % t for t in range(4)]
    + ["ZL%d" % t for t in range(4)] + ["ZR%d" % t for t in range(4)]
    + ["XS%d" % t for t in range(3)]
    + ["XL0", "XR0", "XL1a", "XL1b", "XR1a", "XR1b"]
    + ["y%d_%d_%d" % (s, k, h) for s in range(4) for k in range(4) for h in range(2)]
    + ["out%d" % s for s in range(4)]
)
RS = {name: at for at, name in enumerate(_NAMES)}


def wrap(v, n):
    return lax.rem(v + n, n)


def select(i, values):
    out = (i == 0).astype(jnp.int32) * values[0]
    for at in range(1, len(values)):
        out = out + (i == at).astype(jnp.int32) * values[at]
    return out


def split(v):
    hi = v.astype(BF16)
    return hi, (v - hi.astype(F32)).astype(BF16)


def view(ref, index):
    return lambda: ref.at[index]


def dot(a, b):
    return jnp.dot(a, b, preferred_element_type=F32)


def kernel(
    feat, proto, counts, fg, pg_out,
    cnt, u, ut, e, ghi, glo, ug, sib, cth, ctl, chi, clo, pg, pgo, sb, own,
    tbuf, t1, t2, t3, ringl, ringr, xs, xb, zl, zr, y1, y2,
    ssem, rsem, t1s, t2s, t3s, t1r, t2r, t3r,
):
    p = lax.axis_index("proto")
    y = lax.axis_index("view")
    c = lax.rem(p, 2)
    x = lax.rem(p // 2, XN)
    z = p // (2 * XN)

    def dev(zz, xx, cc):
        return {"proto": (zz * XN + xx) * 2 + cc}

    sibling = dev(z, x, 1 - c)
    right_z, left_z = dev(wrap(z + 1, ZN), x, c), dev(wrap(z - 1, ZN), x, c)
    right_x, left_x = dev(z, wrap(x + 1, XN), c), dev(z, wrap(x - 1, XN), c)
    far_x = dev(z, wrap(x + 2, XN), c)
    y0, yb1 = lax.rem(y, 2), y // 2
    mate_a = {"view": yb1 * 2 + (1 - y0)}
    mate_b = {"view": (1 - yb1) * 2 + (1 - y0)}
    fbit, gbit = lax.rem(y0 + yb1, 2), yb1

    g8 = lax.rem(p, 8)
    peers = [dict(proto=z * 8 + lax.rem(g8 + k, 8)) for k in range(1, 8)]
    ranks = [lax.rem(g8 + k, 8) for k in range(1, 8)]
    zpeers = [dev(lax.rem(z + k, ZN), x, c) for k in range(1, 8)]

    cnt_copy = pltpu.make_async_copy(counts, cnt, rsem.at[RS["cnt"]])
    cnt_copy.start()
    pro_copy = pltpu.make_async_copy(proto, pg, rsem.at[RS["pro"]])
    pro_copy.start()

    barrier = pltpu.get_barrier_semaphore()
    for d in peers + zpeers + [mate_a, mate_b]:
        pl.semaphore_signal(barrier, inc=1, device_id=d, device_id_type=MESH)

    sent = [[], [], []]

    def send(who, src, dst, name, device):
        at = len(sent[who]) + (0 if who < 2 else 64)

        def make():
            return pltpu.make_async_remote_copy(
                src_ref=src() if callable(src) else src, dst_ref=dst() if callable(dst) else dst,
                send_sem=ssem.at[at], recv_sem=rsem.at[RS[name]],
                device_id=device, device_id_type=MESH,
            )

        sent[who].append(make)
        make().start()

    def arrive(dst, name):
        pltpu.make_async_remote_copy(
            src_ref=dst, dst_ref=dst, send_sem=ssem.at[0], recv_sem=rsem.at[RS[name]],
            device_id=sibling, device_id_type=MESH,
        ).wait_recv()

    q_of = {}
    for name in ORDER:
        if name[0] == "A":
            q_of[name] = wrap(z + name[1], ZN)
        else:
            q_of[name] = 8 + wrap(x + name[1], XN) * 2 + name[2]
    at_of = {name: pl.multiple_of(q * CH, CH) for name, q in q_of.items()}

    def urows(name, lo=0, n=CH):
        return u.at[pl.ds(pl.multiple_of(at_of[name] + lo, 8), n)]

    def ublk(dz):
        return u.at[pl.ds(pl.multiple_of(ROWS // 2 + x * 2 * CH + wrap(z + dz, ZN) * BLK, 8), BLK)]

    def ublk_half(dz, h):
        at = ROWS // 2 + x * 2 * CH + wrap(z + dz, ZN) * BLK + h * (BLK // 2)
        return u.at[pl.ds(pl.multiple_of(at, 8), BLK // 2)]

    def ublk_a(dx):
        return u.at[pl.ds(pl.multiple_of(z * CH + wrap(x + dx, XN) * BLK, 8), BLK)]

    own_at = pl.multiple_of(
        jnp.where(c == 0, z * CH + x * BLK, ROWS // 2 + x * 2 * CH + z * BLK), 8
    )
    own_a, blocks_a = ublk_a(0), [ublk_a(-1), ublk_a(1), ublk_a(2)]
    blk = {d: ublk(d) for d in range(-3, 4)}
    half4 = [ublk_half(4, 0), ublk_half(4, 1)]
    halfm3, halfp3 = ublk_half(-3, 0), ublk_half(3, 1)
    rows = {name: urows(name) for name in ORDER}
    a4h = [urows(("A", 4), 0, CH // 2), urows(("A", 4), CH // 2, CH // 2)]
    am3h, ap3h = urows(("A", -3), 0, CH // 2), urows(("A", 3), CH // 2, CH // 2)

    def load_features():
        crops = []
        for j in range(2):
            crops.append(jnp.concatenate([feat[pl.ds(kt * 2 + j, BLK // 2, stride=4), :] for kt in range(2)], axis=1))
        f = jnp.concatenate(crops, axis=0)
        norm = jnp.sqrt(jnp.sum(f * f, axis=1, keepdims=True) + 1e-6)
        return f, norm

    f, norm = load_features()
    u[pl.ds(own_at, BLK), :] = f / norm

    pl.semaphore_wait(barrier, 16)

    @pl.when(c == 0)
    def _():
        send(0, own_a, own_a, "x0", right_x)
        send(0, own_a, own_a, "x1", left_x)
        send(0, own_a, own_a, "x2", far_x)

    @pl.when(c == 1)
    def _():
        send(1, blk[0], blk[0], "bl1", right_z)
        send(1, blk[0], blk[0], "br1", left_z)

    pro_copy.wait()

    def centroids(i, carry):
        at = pl.multiple_of(i * 256, 256)
        v = pg[pl.ds(at, 256), :]
        v = v / jnp.sqrt(jnp.sum(v * v, axis=1, keepdims=True) + 1e-6)
        hi, lo = split(v)
        chi[pl.ds(at, 256), :] = hi
        clo[pl.ds(at, 256), :] = lo
        hi, lo = split(jnp.transpose(v * SCORE_SCALE))
        cth[:, pl.ds(at, 256)] = hi
        ctl[:, pl.ds(at, 256)] = lo
        return carry

    lax.fori_loop(0, KL // 256, centroids, 0)
    tbuf[...] = jnp.zeros_like(tbuf)
    eye = lax.broadcasted_iota(jnp.int32, (CH // 2, 128), 0) == lax.broadcasted_iota(jnp.int32, (CH // 2, 128), 1)

    def core1_ring(t):
        if t < 4:
            arrive(blk[-t], "bl%d" % t)
            arrive(blk[t], "br%d" % t)
        else:
            arrive(half4[0], "bl4")
            arrive(half4[1], "br4")
        if t < 3:
            send(1, blk[-t], blk[-t], "bl%d" % (t + 1), right_z)
            send(1, blk[t], blk[t], "br%d" % (t + 1), left_z)
        elif t == 3:
            send(1, halfm3, halfm3, "bl4", right_z)
            send(1, halfp3, halfp3, "br4", left_z)

    def stage_a(t):
        if t < 4:
            left, right = rows[("A", -t)], rows[("A", t)]
        else:
            left, right = a4h
        arrive(left, "al%d" % t)
        arrive(right, "ar%d" % t)

        @pl.when(c == 0)
        def _():
            if t < 3:
                send(0, left, left, "al%d" % (t + 1), right_z)
                send(0, right, right, "ar%d" % (t + 1), left_z)
            elif t == 3:
                send(0, am3h, am3h, "al4", right_z)
                send(0, ap3h, ap3h, "ar4", left_z)
            send(0, left, left, "al%d" % t, sibling)
            send(0, right, right, "ar%d" % t, sibling)

    def stage_b(name, at, onward=None):
        arrive(rows[name], "b%d" % at)

        @pl.when(c == 1)
        def _():
            if onward is not None:
                send(1, rows[name], rows[name], "b%d" % onward[0], onward[1])
            send(1, rows[name], rows[name], "b%d" % at, sibling)

    def gather_comm(i):
        if i == 0:
            @pl.when(c == 0)
            def _():
                for k in range(3):
                    arrive(blocks_a[k], "x%d" % k)
                r = rows[("A", 0)]
                send(0, r, r, "al1", right_z)
                send(0, r, r, "ar1", left_z)
                send(0, r, r, "a0", sibling)

            @pl.when(c == 1)
            def _():
                for t in (1, 2, 3):
                    core1_ring(t)
                arrive(rows[("A", 0)], "a0")

            stage_a(1)
        elif i == 1:
            @pl.when(c == 1)
            def _():
                core1_ring(4)
                ra, rb = rows[("B", 0, 0)], rows[("B", 0, 1)]
                send(1, ra, ra, "b2", right_x)
                send(1, rb, rb, "b5", left_x)
                send(1, rb, rb, "b3", right_x)
                send(1, ra, ra, "b4", left_x)
                send(1, ra, ra, "b0", sibling)
                send(1, rb, rb, "b1", sibling)

            stage_a(2)
        elif i == 2:
            @pl.when(c == 0)
            def _():
                arrive(rows[("B", 0, 0)], "b0")
                arrive(rows[("B", 0, 1)], "b1")
        elif i == 3:
            stage_a(3)
        elif i == 4:
            stage_b(("B", -1, 0), 2, (6, right_x))
        elif i == 5:
            stage_b(("B", 1, 1), 5, (7, left_x))
            stage_a(4)
        elif i == 6:
            stage_b(("B", -1, 1), 3)
            stage_b(("B", 1, 0), 4)
        elif i == 7:
            stage_b(("B", 2, 0), 6)
            stage_b(("B", 2, 1), 7)

    def source(q, k):
        over = q - 8
        return jnp.where(q < 8, q * 8 + 2 * k, (lax.rem(over + 8, 2) * 4 + k) * 8 + (over + 8) // 2 * 2 - 8 + 1)

    def counts_at(first, kt):
        return jnp.concatenate(
            [cnt[pl.ds(first + (kt * 2 + 1 - j), BLK // 2, stride=16), :] for j in range(2)], axis=0
        )

    qs = [q_of[name] for name in ORDER]

    def forward(i, carry):
        for k in range(8):
            @pl.when(i == k)
            def _(k=k):
                gather_comm(k)

        q2 = [select(i, qs[h::2]) for h in range(2)]
        v = jnp.concatenate([u[pl.ds(pl.multiple_of(q * CH, 8), CH), :] for q in q2], axis=0)
        hi, lo = split(v)
        at = pl.multiple_of(i * 2 * CH, 2 * CH)
        part = None
        for n in range(4):
            cols = pl.ds(n * 256, 256)
            s = dot(hi, cth[:, cols]) + dot(lo, cth[:, cols]) + dot(hi, ctl[:, cols])
            ex = jnp.exp2(s)
            e[pl.ds(at, 2 * CH), cols] = ex
            two = ex[:, :128] + ex[:, 128:]
            part = two if part is None else part + two
        total = jnp.sum(part, axis=1, keepdims=True)
        hi, lo = split(jnp.transpose(v))
        ut[0:D, pl.ds(at, 2 * CH)] = hi
        ut[D : 2 * D, pl.ds(at, 2 * CH)] = lo
        for h in range(2):
            for k in range(2):
                col = total[h * CH + k * (CH // 2) : h * CH + (k + 1) * (CH // 2)]
                row = jnp.sum(jnp.where(eye, col, 0.0), axis=0, keepdims=True)
                tbuf[q2[h], k : k + 1, :] = row
                masses = []
                for b in range(2):
                    first = source(q2[h], 2 * k + b) * (BLK // 2 * 16)
                    m = counts_at(first, 0)
                    for kt in range(1, 8):
                        m = m + counts_at(first, kt)
                    masses.append(m.astype(F32))
                col = jnp.sum(jnp.concatenate(masses, axis=0), axis=1, keepdims=True)
                row = jnp.sum(jnp.where(eye, col, 0.0), axis=0, keepdims=True)
                tbuf[q2[h], 2 + k : 3 + k, :] = row
        return carry

    cnt_copy.wait()
    lax.fori_loop(0, 8, forward, 0)

    def small(src, dst, ss, rr, device):
        return pltpu.make_async_remote_copy(
            src_ref=src, dst_ref=dst, send_sem=ss, recv_sem=rr, device_id=device, device_id_type=MESH
        )

    def eighth(buf, r):
        return buf.at[pl.ds(pl.multiple_of(r * 2, 2), 2)]

    first = [small(eighth(tbuf, ranks[k]), t1.at[k], t1s.at[k], t1r.at[k], peers[k]) for k in range(7)]
    for copy in first:
        copy.start()
    for copy in first:
        copy.wait()
    mine = tbuf[pl.ds(g8 * 2, 2)]
    for k in range(7):
        mine = mine + t1[k]
    t2[7] = mine
    second = [small(t2.at[7], t2.at[k], t2s.at[k], t2r.at[k], zpeers[k]) for k in range(7)]
    for copy in second:
        copy.start()
    for copy in second:
        copy.wait()
    mine = t2[7]
    for k in range(7):
        mine = mine + t2[k]
    ratio = (mine[:, 2:4, :] * (FIXED_POINT * WEIGHT)) / jnp.maximum(mine[:, 0:2, :], 1e-30)
    t3[pl.ds(g8 * 2, 2), 0:2, :] = ratio
    third = [small(eighth(t3, g8), eighth(t3, g8), t3s.at[k], t3r.at[k], peers[k]) for k in range(7)]
    for copy in third:
        copy.start()
    for k in range(7):
        small(eighth(t3, ranks[6 - k]), eighth(t3, ranks[6 - k]), t3s.at[k], t3r.at[k], peers[k]).wait_recv()
    for copy in third:
        copy.wait_send()

    def spread(pos, carry):
        q = select(pos, qs)
        for k in range(2):
            row = t3[q, k : k + 1, :]
            col = jnp.sum(jnp.where(eye, row, 0.0), axis=1, keepdims=True)
            at = pl.multiple_of(pos * CH + k * (CH // 2), 8)
            sb[pl.ds(at, CH // 2), :] = jnp.broadcast_to(col, (CH // 2, 128))
        return carry

    lax.fori_loop(0, NC, spread, 0)

    def ypart(s):
        h1, h2 = s * 256, s * 256 + 128

        def ds(at, n):
            return pl.ds(pl.multiple_of(at, 8), n)

        return dict(
            away1=(ds(h1 + (1 - fbit) * 64, 64), ds(h2 + (1 - gbit) * 64, 64)),
            keep1=(ds(h1 + fbit * 64, 64), ds(h2 + gbit * 64, 64)),
            away2=(ds(h1 + fbit * 64 + (1 - gbit) * 32, 32), ds(h2 + gbit * 64 + (1 - fbit) * 32, 32)),
            keep2=(ds(h1 + fbit * 64 + gbit * 32, 32), ds(h2 + gbit * 64 + fbit * 32, 32)),
        )

    yparts = [ypart(s) for s in range(4)]

    def out_copy(s):
        rng = pl.ds(s * 256, 256)
        return pltpu.make_async_copy(pgo.at[rng], pg_out.at[rng], rsem.at[RS["out%d" % s]])

    def ystep(k, s):
        part = yparts[s]
        for h in range(2):
            near, far = (mate_a, mate_b) if h == 0 else (mate_b, mate_a)
            name = "y%d_%d_%d" % (s, k - 1, h)
            prev = "y%d_%d_%d" % (s, k - 2, h)
            if k == 1:
                send(2, view(pg, (part["away1"][h],)), view(y1, (s, h,)), name, near)
            elif k == 2:
                arrive(y1.at[s, h], prev)
                keep = part["keep1"][h]
                pg[keep, :] = pg[keep, :] + y1[s, h]
                send(2, view(pg, (part["away2"][h],)), view(y2, (s, h,)), name, far)
            elif k == 3:
                arrive(y2.at[s, h], prev)
                keep = part["keep2"][h]
                pgo[keep, :] = pg[keep, :] + y2[s, h]
                send(2, view(pgo, (keep,)), view(pgo, (keep,)), name, far)
            elif k == 4:
                arrive(pgo.at[part["away2"][h]], prev)
                send(2, view(pgo, (part["keep1"][h],)), view(pgo, (part["keep1"][h],)), name, near)
            elif k == 5:
                arrive(pgo.at[part["away1"][h]], prev)
        if k == 5:
            out_copy(s).start()

    def slab(s, carry):
        col = pl.multiple_of(s * 256, 256)

        def gradient(pos, carry):
            q = select(pos, qs)
            for k in range(4):
                first = source(q, k) * (BLK // 2 * 16) + s * 4
                at = pl.ds(pl.multiple_of(pos * CH + k * BLK, 16), BLK)
                w = sb[at, :]
                for kt in range(2):
                    cols = pl.ds(pl.multiple_of(col + kt * 128, 128), 128)
                    g = w * e[at, cols] - counts_at(first, kt).astype(F32) * (FIXED_POINT * WEIGHT)
                    hi, lo = split(g)
                    ghi[at, cols] = hi
                    glo[at, cols] = lo
            return carry

        lax.fori_loop(0, NC, gradient, 0)
        cols = pl.ds(col, 256)
        both = dot(ut[...], ghi[:, cols])
        acc = both[:D] + both[D:] + dot(ut[0:D, :], glo[:, cols])
        pg[cols, :] = jnp.transpose(acc)
        for k in range(4):
            @pl.when(s == k)
            def _(k=k):
                for t in range(k + 1):
                    ystep(t + 1, k - t)
        return carry

    lax.fori_loop(0, 4, slab, 0)

    def grows(name, lo=0, n=CH):
        return pl.ds(POS[name] * CH + lo, n)

    def add(dst, buf, src):
        ug[dst, :] = ug[dst, :] + buf[src, :]

    def to_sibling(names):
        for kind in "AB":
            mine = [n for n in names if n[0] == kind]
            if not mine:
                continue
            who = 1 if kind == "A" else 0

            @pl.when(c == who)
            def _():
                for n in mine:
                    send(who, view(ug, (grows(n),)), view(sib, (SIB[n],)), "s%d" % SIB[n], sibling)

    def from_sibling(name):
        arrive(sib.at[SIB[name]], "s%d" % SIB[name])
        ug[grows(name), :] = ug[grows(name), :] + sib[SIB[name]]

    half = CH // 2
    ring_at = [(0, half), (half, CH), (half + CH, CH), (half + 2 * CH, CH)]

    def core0_stage(d):
        if d == 4:
            from_sibling(("A", 4))
            rng = pl.ds(0, half)
            send(0, view(ug, (grows(("A", 4), 0, half),)), view(ringl, (rng,)), "L0", left_z)
            send(0, view(ug, (grows(("A", 4), half, half),)), view(ringr, (rng,)), "R0", right_z)
            return
        lo, n = ring_at[3 - d]
        src, nxt = pl.ds(lo, n), pl.ds(*ring_at[4 - d])
        for sign, buf, tag, to in ((-1, ringl, "L", left_z), (1, ringr, "R", right_z)):
            name = ("A", sign * d)
            from_sibling(name)
            arrive(buf.at[src], "%s%d" % (tag, 3 - d))
            off = half if (d == 3 and sign == 1) else 0
            add(grows(name, off, n), buf, src)
            send(0, view(ug, (grows(name),)), view(buf, (nxt,)), "%s%d" % (tag, 4 - d), to)

    def core0_last():
        from_sibling(("A", 0))
        src = pl.ds(*ring_at[3])
        arrive(ringl.at[src], "L3")
        add(grows(("A", 0)), ringl, src)
        arrive(ringr.at[src], "R3")
        add(grows(("A", 0)), ringr, src)

    base_a = POS[("A", 0)] * CH
    xblock = [pl.ds(pl.multiple_of(base_a + wrap(x + dx, XN) * BLK, 8), BLK) for dx in range(4)]
    xdev = [dev(z, wrap(x + dx, XN), c) for dx in range(4)]

    def core0_x():
        for dx in (1, 2, 3):
            send(0, view(ug, (xblock[dx],)), view(xs, (dx - 1,)), "XS%d" % (dx - 1), xdev[dx])

    def core0_end():
        total = ug[xblock[0], :]
        for dx in (1, 2, 3):
            arrive(xs.at[dx - 1], "XS%d" % (dx - 1))
            total = total + xs[dx - 1]
        own[...] = total

    xbr = [pl.ds(k * CH, CH) for k in range(6)]

    def core1_first():
        from_sibling(("B", 2, 0))
        send(1, view(ug, (grows(("B", 2, 0)),)), view(xb, (xbr[0],)), "XL0", left_x)
        from_sibling(("B", 2, 1))
        send(1, view(ug, (grows(("B", 2, 1)),)), view(xb, (xbr[1],)), "XR0", right_x)

    def core1_near():
        for name, src, tag, dst, out, to in (
            (("B", -1, 0), 0, "XL0", 2, "XL1a", left_x),
            (("B", 1, 1), 1, "XR0", 4, "XR1b", right_x),
        ):
            from_sibling(name)
            arrive(xb.at[xbr[src]], tag)
            add(grows(name), xb, xbr[src])
            send(1, view(ug, (grows(name),)), view(xb, (xbr[dst],)), out, to)

    def core1_near2():
        for name, dst, out, to in (
            (("B", -1, 1), 3, "XL1b", left_x),
            (("B", 1, 0), 5, "XR1a", right_x),
        ):
            from_sibling(name)
            send(1, view(ug, (grows(name),)), view(xb, (xbr[dst],)), out, to)

    def core1_own():
        for name, pair in ((("B", 0, 0), ((2, "XL1a"), (5, "XR1a"))), (("B", 0, 1), ((3, "XL1b"), (4, "XR1b")))):
            from_sibling(name)
            for src, tag in pair:
                arrive(xb.at[xbr[src]], tag)
                add(grows(name), xb, xbr[src])

    base_b = POS[("B", 0, 0)] * CH

    def gblk(dz, lo=0, n=BLK):
        return pl.ds(pl.multiple_of(base_b + wrap(z + dz, ZN) * BLK + lo, 8), n)

    gb = {d: gblk(d) for d in range(-3, 4)}
    hb = BLK // 2
    gh = {(4, 0): gblk(4, 0, hb), (4, 1): gblk(4, hb, hb), (-3, 0): gblk(-3, 0, hb), (3, 1): gblk(3, hb, hb)}
    zat = [pl.ds(0, hb), pl.ds(hb, BLK), pl.ds(hb + BLK, BLK), pl.ds(hb + 2 * BLK, BLK)]

    def core1_z(d):
        if d == 4:
            send(1, view(ug, (gh[(4, 0)],)), view(zl, (zat[0],)), "ZL0", left_z)
            send(1, view(ug, (gh[(4, 1)],)), view(zr, (zat[0],)), "ZR0", right_z)
            return
        for sign, buf, tag, to in ((-1, zl, "ZL", left_z), (1, zr, "ZR", right_z)):
            src, nxt = zat[3 - d], zat[4 - d]
            arrive(buf.at[src], "%s%d" % (tag, 3 - d))
            dst = gh[(sign * 3, 0 if sign < 0 else 1)] if d == 3 else gb[sign * d]
            add(dst, buf, src)
            send(1, view(ug, (gb[sign * d],)), view(buf, (nxt,)), "%s%d" % (tag, 4 - d), to)

    def core1_end():
        arrive(zl.at[zat[3]], "ZL3")
        arrive(zr.at[zat[3]], "ZR3")
        own[...] = ug[gb[0], :] + zl[zat[3], :] + zr[zat[3], :]

    def on(who, *steps):
        @pl.when(c == who)
        def _():
            for step in steps:
                step()

    def back_comm(i):
        to_sibling(BACK[2 * i : 2 * i + 2])
        if i == 0:
            ystep(2, 3), ystep(3, 2), ystep(4, 1)
        elif i == 1:
            on(1, core1_first)
            ystep(5, 0)
        elif i == 2:
            on(0, lambda: core0_stage(4))
            ystep(3, 3), ystep(4, 2)
        elif i == 3:
            on(0, lambda: core0_stage(3))
        elif i == 4:
            on(1, core1_near)
            ystep(4, 3), ystep(5, 1)
        elif i == 5:
            on(1, core1_near2)
        elif i == 6:
            on(0, lambda: core0_stage(2))
        elif i == 7:
            on(0, lambda: core0_stage(1))

    back = [POS[name] for name in BACK]

    def backward(i, carry):
        at = [pl.multiple_of(select(i, back[h::2]) * CH, CH) for h in range(2)]
        hi = jnp.concatenate([ghi[pl.ds(a, CH), :] for a in at], axis=0)
        lo = jnp.concatenate([glo[pl.ds(a, CH), :] for a in at], axis=0)
        grad = dot(hi, chi[...]) + dot(hi, clo[...]) + dot(lo, chi[...])
        for h in range(2):
            ug[pl.ds(at[h], CH), :] = grad[h * CH : (h + 1) * CH]
        for k in range(8):
            @pl.when(i == k)
            def _(k=k):
                back_comm(k)
        return carry

    lax.fori_loop(0, 8, backward, 0)

    on(0, core0_last, core0_x)
    on(1, core1_own, lambda: core1_z(4), lambda: core1_z(3), lambda: core1_z(2), lambda: core1_z(1))
    on(0, core0_end)
    on(1, core1_end)

    f, norm = load_features()
    unit = f / norm
    grad = own[...]
    inner = jnp.sum(unit * grad, axis=1, keepdims=True)
    out = (grad - unit * inner) / norm
    for j in range(2):
        for kt in range(2):
            piece = out[j * (BLK // 2) : (j + 1) * (BLK // 2), kt * 128 : (kt + 1) * 128]
            fg[pl.ds(kt * 2 + j, BLK // 2, stride=4), :] = piece

    ystep(5, 2)
    ystep(5, 3)
    for who in (0, 1):
        @pl.when(c == who)
        def _(who=who):
            for make in sent[who]:
                make().wait_send()
    for make in sent[2]:
        make().wait_send()
    for s in range(4):
        out_copy(s).wait()


def per_device(features, prototypes, code_counts):
    feat = features.reshape(24, 2, 2, 128).transpose(0, 2, 1, 3).reshape(96, 128)
    counts = code_counts.reshape(1536, 2, 8, 128).transpose(0, 2, 1, 3).reshape(1536 * 16, 128)
    vmem, hbm = pl.BlockSpec(memory_space=pltpu.VMEM), pl.BlockSpec(memory_space=pl.ANY)
    half = CH // 2
    dma = pltpu.SemaphoreType.DMA
    fg, pg = pl.pallas_call(
        kernel,
        out_shape=(jax.ShapeDtypeStruct((96, 128), F32), jax.ShapeDtypeStruct((KL, D), F32)),
        in_specs=[vmem, hbm, hbm],
        out_specs=(vmem, hbm),
        scratch_shapes=[
            pltpu.VMEM((1536 * 16, 128), jnp.int32),
            pltpu.VMEM((ROWS, D), F32),
            pltpu.VMEM((2 * D, ROWS), BF16),
            pltpu.VMEM((ROWS, KL), F32),
            pltpu.VMEM((ROWS, KL), BF16),
            pltpu.VMEM((ROWS, KL), BF16),
            pltpu.VMEM((ROWS, D), F32),
            pltpu.VMEM((8, CH, D), F32),
            pltpu.VMEM((D, KL), BF16),
            pltpu.VMEM((D, KL), BF16),
            pltpu.VMEM((KL, D), BF16),
            pltpu.VMEM((KL, D), BF16),
            pltpu.VMEM((KL, D), F32),
            pltpu.VMEM((KL, D), F32),
            pltpu.VMEM((ROWS, 128), F32),
            pltpu.VMEM((BLK, D), F32),
            pltpu.VMEM((NC, 8, 128), F32),
            pltpu.VMEM((7, 2, 8, 128), F32),
            pltpu.VMEM((8, 2, 8, 128), F32),
            pltpu.VMEM((NC, 8, 128), F32),
            pltpu.VMEM((half + 3 * CH, D), F32),
            pltpu.VMEM((half + 3 * CH, D), F32),
            pltpu.VMEM((3, BLK, D), F32),
            pltpu.VMEM((6 * CH, D), F32),
            pltpu.VMEM((BLK // 2 + 3 * BLK, D), F32),
            pltpu.VMEM((BLK // 2 + 3 * BLK, D), F32),
            pltpu.VMEM((4, 2, 64, D), F32),
            pltpu.VMEM((4, 2, 32, D), F32),
            dma((96,)),
            dma((len(RS),)),
            dma((7,)), dma((7,)), dma((7,)), dma((7,)), dma((7,)), dma((7,)),
        ],
        compiler_params=pltpu.CompilerParams(
            collective_id=0, has_side_effects=True, vmem_limit_bytes=60 << 20
        ),
        cost_estimate=pl.CostEstimate(flops=18 * ROWS * KL * D, bytes_accessed=16 << 20, transcendentals=ROWS * KL),
    )(feat, prototypes, counts)
    features_grad = fg.reshape(24, 2, 2, 128).transpose(0, 2, 1, 3).reshape(24, 2, 256)
    return features_grad, pg


def solution(mesh):
    in_specs = (P(("view", "proto"), None, None), P("proto", None), P("view", None, "proto"))
    out_specs = (P(("view", "proto"), None, None), P("proto", None))
    return jax.shard_map(
        per_device, mesh=mesh, in_specs=in_specs, out_specs=out_specs, check_vma=False
    )
```

```python
import jax
import jax.numpy as jnp
from jax import lax
from jax.experimental import pallas as pl
from jax.experimental.pallas import tpu as pltpu
from jax.sharding import PartitionSpec as P

MESH = pl.DeviceIdType.MESH
F32 = jnp.float32
BF16 = jnp.bfloat16
WEIGHT = 4096.0 / 0.1
FIXED_POINT = 2.0 ** (-24)
SCORE_SCALE = 10.0 * 1.4426950408889634

D = 256
KL = 1024
BLK = 48
HALF = 4 * BLK
GRP = 2 * HALF
ROWS = 8 * GRP
ZN, XN = 8, 4

ORDER = [0, 1, 7, 2, 6, 3, 5, 4]
POS = {dz: at for at, dz in enumerate(ORDER)}
BACK = [4, 3, 5, 2, 6, 1, 7, 0]
FAR = [4, 3, 5, 2, 6]

_NAMES = (
    ["pro"]
    + ["px%d" % d for d in range(1, 4)] + ["pz%d" % d for d in range(1, 8)]
    + ["rz%d_%d" % (d, k) for d in (1, 7) for k in range(1, 4)]
    + ["rx%d_%d" % (d, k) for d in range(2, 7) for k in range(1, 4)]
    + ["s%d" % d for d in range(8)] + ["q%d" % d for d in range(8)]
    + ["gx%d_%d" % (d, k) for d in range(2, 7) for k in range(1, 4)]
    + ["gn1", "gn7"] + ["gz%d" % d for d in range(2, 7)] + ["hx%d" % d for d in range(1, 4)]
    + ["y%d_%d_%d" % (s, k, h) for s in range(4) for k in range(4) for h in range(2)]
    + ["out%d" % s for s in range(4)]
)
RS = {name: at for at, name in enumerate(_NAMES)}


def wrap(v, n):
    return lax.rem(v + n, n)


def select(i, values):
    out = (i == 0).astype(jnp.int32) * values[0]
    for at in range(1, len(values)):
        out = out + (i == at).astype(jnp.int32) * values[at]
    return out


def split(v):
    hi = v.astype(BF16)
    return hi, (v - hi.astype(F32)).astype(BF16)


def view(ref, index):
    return lambda: ref.at[index]


def dot(a, b):
    return jnp.dot(a, b, preferred_element_type=F32)


def kernel(
    feat, proto, counts, fg, pg_out,
    cnt, u, ut, utw, ehi, elo, qhi, qlo, ec, ug, sib, cth, ctl, chi, clo, pg, pgo, own,
    tbuf, t1, t2, t3, gxb, gnb, gzb, hxb, y1, y2,
    ssem, rsem, cntsem, t1s, t2s, t3s, t1r, t2r, t3r,
):
    p = lax.axis_index("proto")
    y = lax.axis_index("view")
    c = lax.rem(p, 2)
    x = lax.rem(p // 2, XN)
    z = p // (2 * XN)

    def dev(zz, xx, cc):
        return {"proto": (zz * XN + xx) * 2 + cc}

    sibling = dev(z, x, 1 - c)
    y0, yb1 = lax.rem(y, 2), y // 2
    mate_a = {"view": yb1 * 2 + (1 - y0)}
    mate_b = {"view": (1 - yb1) * 2 + (1 - y0)}
    fbit, gbit = lax.rem(y0 + yb1, 2), yb1

    g8 = lax.rem(p, 8)
    peers = [dict(proto=z * 8 + lax.rem(g8 + k, 8)) for k in range(1, 8)]
    ranks = [lax.rem(g8 + k, 8) for k in range(1, 8)]
    zpeers = [dev(lax.rem(z + k, ZN), x, c) for k in range(1, 8)]
    xpeers = [dev(z, lax.rem(x + k, XN), c) for k in range(1, 4)]

    pro_copy = pltpu.make_async_copy(proto, pg, rsem.at[RS["pro"]])
    pro_copy.start()

    barrier = pltpu.get_barrier_semaphore()
    for d in peers + zpeers + [mate_a, mate_b]:
        pl.semaphore_signal(barrier, inc=1, device_id=d, device_id_type=MESH)

    sent = []

    def send(src, dst, name, device):
        at = len(sent)

        def make():
            return pltpu.make_async_remote_copy(
                src_ref=src() if callable(src) else src, dst_ref=dst() if callable(dst) else dst,
                send_sem=ssem.at[at], recv_sem=rsem.at[RS[name]],
                device_id=device, device_id_type=MESH,
            )

        sent.append(make)
        make().start()

    def arrive(dst, name):
        pltpu.make_async_remote_copy(
            src_ref=dst, dst_ref=dst, send_sem=ssem.at[0], recv_sem=rsem.at[RS[name]],
            device_id=sibling, device_id_type=MESH,
        ).wait_recv()

    zs = [lax.rem(z + d, ZN) for d in range(8)]
    qs = [zs[d] for d in ORDER]

    def ublk(dz, dx):
        return u.at[pl.ds(pl.multiple_of(zs[dz] * GRP + c * HALF + lax.rem(x + dx, XN) * BLK, 8), BLK)]

    def uhalf(dz, core):
        return u.at[pl.ds(pl.multiple_of(zs[dz] * GRP + core * HALF, 8), HALF)]

    blk = {(dz, dx): ublk(dz, dx) for dz in range(8) for dx in range(4)}
    mine_of = [uhalf(dz, c) for dz in range(8)]
    theirs_of = [uhalf(dz, 1 - c) for dz in range(8)]
    own_at = pl.multiple_of(zs[0] * GRP + c * HALF + x * BLK, 8)
    vb = BLK // 2 * 16

    def count_copies(i):
        slot = lax.rem(i, 3)
        copies = []
        group = select(i, qs)
        for b in range(8):
            owner = group * 8 + (b % 4) * 2 + b // 4
            copies.append(
                pltpu.make_async_copy(
                    counts.at[pl.ds(pl.multiple_of(owner * vb, vb), vb)],
                    cnt.at[slot, pl.ds(b * vb, vb)],
                    cntsem.at[slot],
                )
            )
        return copies

    def fetch(i, carry):
        for copy in count_copies(i):
            copy.start()
        return carry

    lax.fori_loop(0, 2, fetch, 0)

    def load_features():
        crops = []
        for j in range(2):
            crops.append(jnp.concatenate([feat[pl.ds(kt * 2 + j, BLK // 2, stride=4), :] for kt in range(2)], axis=1))
        f = jnp.concatenate(crops, axis=0)
        norm = jnp.sqrt(jnp.sum(f * f, axis=1, keepdims=True) + 1e-6)
        return f, norm

    f, norm = load_features()
    u[pl.ds(own_at, BLK), :] = f / norm

    pl.semaphore_wait(barrier, 16)

    own_blk = blk[0, 0]
    for d in (1, 3, 2):
        send(own_blk, own_blk, "px%d" % d, xpeers[d - 1])
    for d in (4, 3, 5, 2, 6, 1, 7):
        send(own_blk, own_blk, "pz%d" % d, zpeers[d - 1])

    pro_copy.wait()

    def centroids(i, carry):
        at = pl.multiple_of(i * 256, 256)
        v = pg[pl.ds(at, 256), :]
        v = v / jnp.sqrt(jnp.sum(v * v, axis=1, keepdims=True) + 1e-6)
        hi, lo = split(v)
        chi[pl.ds(at, 256), :] = hi
        clo[pl.ds(at, 256), :] = lo
        hi, lo = split(jnp.transpose(v * SCORE_SCALE))
        cth[:, pl.ds(at, 256)] = hi
        ctl[:, pl.ds(at, 256)] = lo
        return carry

    lax.fori_loop(0, KL // 256, centroids, 0)
    tbuf[...] = jnp.zeros_like(tbuf)
    eye = lax.broadcasted_iota(jnp.int32, (128, 128), 0) == lax.broadcasted_iota(jnp.int32, (128, 128), 1)

    def to_rows(col, at, first):
        for k in range(3):
            row = jnp.sum(jnp.where(eye, col[k * 128 : (k + 1) * 128], 0.0), axis=0, keepdims=True)
            tbuf[at, first + k : first + k + 1, :] = row

    def relay_z():
        for d in (1, 2, 3):
            arrive(blk[0, 4 - d], "px%d" % d)
        for d in (1, 2, 3):
            send(blk[0, d], blk[0, d], "rz1_%d" % d, zpeers[0])
            send(blk[0, d], blk[0, d], "rz7_%d" % d, zpeers[6])
        send(mine_of[0], mine_of[0], "s0", sibling)

    def relay_x(dz):
        b = blk[dz, 0]
        arrive(b, "pz%d" % (8 - dz))
        for d in (1, 3, 2):
            send(b, b, "rx%d_%d" % (dz, d), xpeers[d - 1])

    def collect(dz):
        if dz in (1, 7):
            arrive(blk[dz, 0], "pz%d" % (8 - dz))
            for d in (1, 2, 3):
                arrive(blk[dz, d], "rz%d_%d" % (8 - dz, d))
        else:
            for d in (1, 2, 3):
                arrive(blk[dz, 4 - d], "rx%d_%d" % (dz, d))
        send(mine_of[dz], mine_of[dz], "s%d" % dz, sibling)

    def use(dz):
        arrive(theirs_of[dz], "s%d" % dz)

    def early_comm(i):
        if i == 3:
            relay_z()
        elif i == 5:
            relay_x(2), relay_x(6)
        elif i == 6:
            relay_x(3), relay_x(5)
        elif i == 7:
            relay_x(4)

    def gather_comm(i):
        if i == 0:
            collect(1), collect(7)
        elif i < 6:
            collect(ORDER[i + 2])
        use(ORDER[i])

    def codes(i, carry):
        for k in range(8):
            @pl.when(i == k)
            def _(k=k):
                early_comm(k)

        slot = lax.rem(i, 3)
        pltpu.make_async_copy(cnt.at[slot], cnt.at[slot], cntsem.at[slot]).wait()

        @pl.when(i < 6)
        def _():
            fetch(i + 2, 0)

        at = pl.multiple_of(i * GRP, GRP)
        sums = []
        for b in range(8):
            rng = pl.ds(pl.multiple_of(at + b * BLK, 16), BLK)
            mass = None
            for kt in range(8):
                v = jnp.concatenate(
                    [cnt[slot, pl.ds(b * vb + kt * 2 + 1 - j, BLK // 2, stride=16), :] for j in range(2)], axis=0
                ).astype(F32)
                mass = v if mass is None else mass + v
                hi, lo = split(v)
                cols = pl.ds(kt * 128, 128)
                qhi[rng, cols] = hi
                qlo[rng, cols] = lo
            sums.append(mass)
        to_rows(jnp.sum(jnp.concatenate(sums, axis=0), axis=1, keepdims=True), select(i, qs), 3)
        rng = pl.ds(at, GRP)
        hi, lo = qhi[rng, :], qlo[rng, :]
        ug[rng, :] = dot(hi, chi[...]) + dot(hi, clo[...]) + dot(lo, chi[...])
        return carry

    def forward(i, carry):
        for k in range(8):
            @pl.when(i == k)
            def _(k=k):
                gather_comm(k)

        group = select(i, qs)
        v = u[pl.ds(pl.multiple_of(group * GRP, 8), GRP), :]
        hi, lo = split(v)
        at = pl.multiple_of(i * GRP, GRP)
        part = None
        for n in range(4):
            cols = pl.ds(n * 256, 256)
            s = dot(hi, cth[:, cols]) + dot(lo, cth[:, cols]) + dot(hi, ctl[:, cols])
            ex = jnp.exp2(s)
            hi_e, lo_e = split(ex)
            ehi[pl.ds(at, GRP), cols] = hi_e
            elo[pl.ds(at, GRP), cols] = lo_e
            two = ex[:, :128] + ex[:, 128:]
            part = two if part is None else part + two
        total = jnp.sum(part, axis=1, keepdims=True)
        hi, lo = split(jnp.transpose(v))
        ut[0:D, pl.ds(at, GRP)] = hi
        ut[D : 2 * D, pl.ds(at, GRP)] = lo
        to_rows(total, group, 0)
        return carry

    lax.fori_loop(0, 8, codes, 0)
    lax.fori_loop(0, 8, forward, 0)

    def small(src, dst, ss, rr, device):
        return pltpu.make_async_remote_copy(
            src_ref=src, dst_ref=dst, send_sem=ss, recv_sem=rr, device_id=device, device_id_type=MESH
        )

    def codes_slab(s):
        cols = pl.ds(s * 256, 256)
        both = dot(ut[...], qhi[:, cols])
        acc = both[:D] + both[D:] + dot(ut[0:D, :], qlo[:, cols])
        pg[cols, :] = jnp.transpose(acc) * (-FIXED_POINT * WEIGHT)

    def forward_grad(i, carry):
        rng = pl.ds(pl.multiple_of(i * GRP, GRP), GRP)
        hi, lo = ehi[rng, :], elo[rng, :]
        ec[rng, :] = dot(hi, chi[...]) + dot(hi, clo[...]) + dot(lo, chi[...])
        return carry

    first = [small(tbuf.at[ranks[k]], t1.at[k], t1s.at[k], t1r.at[k], peers[k]) for k in range(7)]
    for copy in first:
        copy.start()
    codes_slab(0)
    codes_slab(1)
    for copy in first:
        copy.wait()
    mine = tbuf[g8]
    for k in range(7):
        mine = mine + t1[k]
    t2[7] = mine
    second = [small(t2.at[7], t2.at[k], t2s.at[k], t2r.at[k], zpeers[k]) for k in range(7)]
    for copy in second:
        copy.start()
    codes_slab(2)
    codes_slab(3)
    lax.fori_loop(0, 2, forward_grad, 0)
    for copy in second:
        copy.wait()
    mine = t2[7]
    for k in range(7):
        mine = mine + t2[k]
    t3[g8, 0:3, :] = mine[3:6, :] * (FIXED_POINT * WEIGHT) / mine[0:3, :]
    third = [small(t3.at[g8], t3.at[g8], t3s.at[k], t3r.at[k], peers[k]) for k in range(7)]
    for copy in third:
        copy.start()
    lax.fori_loop(2, 8, forward_grad, 0)
    for k in range(7):
        small(t3.at[ranks[6 - k]], t3.at[ranks[6 - k]], t3s.at[k], t3r.at[k], peers[k]).wait_recv()
    for copy in third:
        copy.wait_send()

    def ypart(s):
        h1, h2 = s * 256, s * 256 + 128

        def ds(at, n):
            return pl.ds(pl.multiple_of(at, 8), n)

        return dict(
            away1=(ds(h1 + (1 - fbit) * 64, 64), ds(h2 + (1 - gbit) * 64, 64)),
            keep1=(ds(h1 + fbit * 64, 64), ds(h2 + gbit * 64, 64)),
            away2=(ds(h1 + fbit * 64 + (1 - gbit) * 32, 32), ds(h2 + gbit * 64 + (1 - fbit) * 32, 32)),
            keep2=(ds(h1 + fbit * 64 + gbit * 32, 32), ds(h2 + gbit * 64 + fbit * 32, 32)),
        )

    yparts = [ypart(s) for s in range(4)]

    def out_copy(s):
        rng = pl.ds(s * 256, 256)
        return pltpu.make_async_copy(pgo.at[rng], pg_out.at[rng], rsem.at[RS["out%d" % s]])

    def ystep(k, s):
        part = yparts[s]
        for h in range(2):
            near, far = (mate_a, mate_b) if h == 0 else (mate_b, mate_a)
            name = "y%d_%d_%d" % (s, k - 1, h)
            prev = "y%d_%d_%d" % (s, k - 2, h)
            if k == 1:
                send(view(pg, (part["away1"][h],)), view(y1, (s, h,)), name, near)
            elif k == 2:
                arrive(y1.at[s, h], prev)
                keep = part["keep1"][h]
                pg[keep, :] = pg[keep, :] + y1[s, h]
                send(view(pg, (part["away2"][h],)), view(y2, (s, h,)), name, far)
            elif k == 3:
                arrive(y2.at[s, h], prev)
                keep = part["keep2"][h]
                pgo[keep, :] = pg[keep, :] + y2[s, h]
                send(view(pgo, (keep,)), view(pgo, (keep,)), name, far)
            elif k == 4:
                arrive(pgo.at[part["away2"][h]], prev)
                send(view(pgo, (part["keep1"][h],)), view(pgo, (part["keep1"][h],)), name, near)
            elif k == 5:
                arrive(pgo.at[part["away1"][h]], prev)
        if k == 5:
            out_copy(s).start()

    def slab(s, carry):
        col = pl.multiple_of(s * 256, 256)

        cols = pl.ds(col, 256)
        both = dot(utw[...], ehi[:, cols])
        acc = both[:D] + both[D:] + dot(utw[0:D, :], elo[:, cols])
        pg[cols, :] = jnp.transpose(acc) + pg[cols, :]
        for k in range(4):
            @pl.when(s == k)
            def _(k=k):
                slab_comm(k)
        return carry

    mine_at = [pl.ds(pl.multiple_of(POS[dz] * GRP + c * HALF, 8), HALF) for dz in range(8)]
    theirs_at = [pl.ds(pl.multiple_of(POS[dz] * GRP + (1 - c) * HALF, 8), HALF) for dz in range(8)]

    def gblk(dz, dx):
        return pl.ds(pl.multiple_of(POS[dz] * GRP + c * HALF + lax.rem(x + dx, XN) * BLK, 8), BLK)

    gb = {(dz, dx): gblk(dz, dx) for dz in range(8) for dx in range(4)}

    def from_sibling(dz):
        arrive(sib.at[dz], "q%d" % dz)
        ug[mine_at[dz], :] = ug[mine_at[dz], :] + sib[dz]

    def sums_out(dz):
        from_sibling(dz)
        if dz in (1, 7):
            send(view(ug, (mine_at[dz],)), view(gnb, (dz // 7,)), "gn%d" % dz, zpeers[dz - 1])
        else:
            for d in (2, 1, 3):
                send(view(ug, (gb[dz, d],)), view(gxb, ((dz - 2) * 3 + d - 1,)), "gx%d_%d" % (dz, d), xpeers[d - 1])

    def sums_onward(dz):
        total = ug[gb[dz, 0], :]
        for d in (1, 2, 3):
            arrive(gxb.at[(dz - 2) * 3 + d - 1], "gx%d_%d" % (dz, d))
            total = total + gxb[(dz - 2) * 3 + d - 1]
        ug[gb[dz, 0], :] = total
        send(view(ug, (gb[dz, 0],)), view(gzb, (dz - 2,)), "gz%d" % dz, zpeers[dz - 1])

    def sums_here():
        from_sibling(0)
        for k, dz in enumerate((1, 7)):
            arrive(gnb.at[k], "gn%d" % dz)
        ug[mine_at[0], :] = ug[mine_at[0], :] + gnb[0] + gnb[1]
        for d in (2, 1, 3):
            send(view(ug, (gb[0, d],)), view(hxb, (d - 1,)), "hx%d" % d, xpeers[d - 1])

    def sums_end():
        total = ug[gb[0, 0], :]
        for d in (1, 2, 3):
            arrive(hxb.at[d - 1], "hx%d" % d)
            total = total + hxb[d - 1]
        for d in (2, 6, 3, 5, 4):
            arrive(gzb.at[d - 2], "gz%d" % d)
            total = total + gzb[d - 2]
        own[...] = total

    def slab_comm(k):
        ystep(1, k)
        if k == 0:
            for dz in BACK[:7]:
                sums_out(dz)
        else:
            if k >= 2:
                ystep(2, k - 2)

    def column(group):
        cols = []
        for k in range(3):
            cols.append(jnp.sum(jnp.where(eye, t3[group, k : k + 1, :], 0.0), axis=1, keepdims=True))
        return jnp.concatenate(cols, axis=0)

    def backward(i, carry):
        rng = pl.ds(pl.multiple_of(select(i, back) * GRP, GRP), GRP)
        w = jnp.broadcast_to(column(select(i, backq)), (GRP, D))
        ug[rng, :] = w * ec[rng, :] - ug[rng, :] * (FIXED_POINT * WEIGHT)
        for k in range(8):
            @pl.when(i == k)
            def _(k=k):
                dz = BACK[k]
                send(view(ug, (theirs_at[dz],)), view(sib, (dz,)), "q%d" % dz, sibling)
        return carry

    def weighted(i, carry):
        group = select(i, qs)
        for k in range(3):
            cols = pl.ds(pl.multiple_of(i * GRP + k * 128, 128), 128)
            v = (ut[0:D, cols].astype(F32) + ut[D : 2 * D, cols].astype(F32)) * t3[group, k : k + 1, :]
            hi, lo = split(v)
            utw[0:D, cols] = hi
            utw[D : 2 * D, cols] = lo
        return carry

    back = [POS[dz] for dz in BACK]
    backq = [zs[dz] for dz in BACK]
    lax.fori_loop(0, 8, backward, 0)
    lax.fori_loop(0, 8, weighted, 0)
    lax.fori_loop(0, 4, slab, 0)

    ystep(2, 2)
    ystep(3, 0)
    sums_here()
    ystep(2, 3)
    ystep(3, 1)
    for dz in FAR:
        sums_onward(dz)
    ystep(3, 2)
    ystep(4, 0)
    ystep(3, 3)
    ystep(4, 1)
    ystep(4, 2)
    ystep(5, 0)
    sums_end()

    f, norm = load_features()
    unit = f / norm
    grad = own[...]
    inner = jnp.sum(unit * grad, axis=1, keepdims=True)
    out = (grad - unit * inner) / norm
    for j in range(2):
        for kt in range(2):
            piece = out[j * (BLK // 2) : (j + 1) * (BLK // 2), kt * 128 : (kt + 1) * 128]
            fg[pl.ds(kt * 2 + j, BLK // 2, stride=4), :] = piece

    ystep(4, 3)
    ystep(5, 1)
    ystep(5, 2)
    ystep(5, 3)
    for make in sent:
        make().wait_send()
    for s in range(4):
        out_copy(s).wait()


def per_device(features, prototypes, code_counts):
    feat = features.reshape(24, 2, 2, 128).transpose(0, 2, 1, 3).reshape(96, 128)
    counts = code_counts.reshape(1536, 2, 8, 128).transpose(0, 2, 1, 3).reshape(1536 * 16, 128)
    vmem, hbm = pl.BlockSpec(memory_space=pltpu.VMEM), pl.BlockSpec(memory_space=pl.ANY)
    dma = pltpu.SemaphoreType.DMA
    fg, pg = pl.pallas_call(
        kernel,
        out_shape=(jax.ShapeDtypeStruct((96, 128), F32), jax.ShapeDtypeStruct((KL, D), F32)),
        in_specs=[vmem, hbm, hbm],
        out_specs=(vmem, hbm),
        scratch_shapes=[
            pltpu.VMEM((3, 8 * BLK // 2 * 16, 128), jnp.int32),
            pltpu.VMEM((ROWS, D), F32),
            pltpu.VMEM((2 * D, ROWS), BF16),
            pltpu.VMEM((2 * D, ROWS), BF16),
            pltpu.VMEM((ROWS, KL), BF16),
            pltpu.VMEM((ROWS, KL), BF16),
            pltpu.VMEM((ROWS, KL), BF16),
            pltpu.VMEM((ROWS, KL), BF16),
            pltpu.VMEM((ROWS, D), F32),
            pltpu.VMEM((ROWS, D), F32),
            pltpu.VMEM((8, HALF, D), F32),
            pltpu.VMEM((D, KL), BF16),
            pltpu.VMEM((D, KL), BF16),
            pltpu.VMEM((KL, D), BF16),
            pltpu.VMEM((KL, D), BF16),
            pltpu.VMEM((KL, D), F32),
            pltpu.VMEM((KL, D), F32),
            pltpu.VMEM((BLK, D), F32),
            pltpu.VMEM((8, 8, 128), F32),
            pltpu.VMEM((7, 8, 128), F32),
            pltpu.VMEM((8, 8, 128), F32),
            pltpu.VMEM((8, 8, 128), F32),
            pltpu.VMEM((15, BLK, D), F32),
            pltpu.VMEM((2, HALF, D), F32),
            pltpu.VMEM((5, BLK, D), F32),
            pltpu.VMEM((3, BLK, D), F32),
            pltpu.VMEM((4, 2, 64, D), F32),
            pltpu.VMEM((4, 2, 32, D), F32),
            dma((128,)),
            dma((len(RS),)),
            dma((3,)),
            dma((7,)), dma((7,)), dma((7,)), dma((7,)), dma((7,)), dma((7,)),
        ],
        compiler_params=pltpu.CompilerParams(
            collective_id=0, has_side_effects=True, vmem_limit_bytes=60 << 20
        ),
        cost_estimate=pl.CostEstimate(flops=18 * ROWS * KL * D, bytes_accessed=16 << 20, transcendentals=ROWS * KL),
    )(feat, prototypes, counts)
    features_grad = fg.reshape(24, 2, 2, 128).transpose(0, 2, 1, 3).reshape(24, 2, 256)
    return features_grad, pg


def solution(mesh):
    in_specs = (P(("view", "proto"), None, None), P("proto", None), P("view", None, "proto"))
    out_specs = (P(("view", "proto"), None, None), P("proto", None))
    return jax.shard_map(
        per_device, mesh=mesh, in_specs=in_specs, out_specs=out_specs, check_vma=False
    )
```

```python
import jax
import jax.numpy as jnp
from jax import lax
from jax.experimental import pallas as pl
from jax.experimental.pallas import tpu as pltpu
from jax.sharding import PartitionSpec as P

MESH = pl.DeviceIdType.MESH
F32 = jnp.float32
BF16 = jnp.bfloat16
WEIGHT = 4096.0 / 0.1
FIXED_POINT = 2.0 ** (-24)
SCORE_SCALE = 10.0 * 1.4426950408889634

D = 256
KL = 1024
BLK = 48
HALF = 4 * BLK
GRP = 2 * HALF
ROWS = 8 * GRP
ZN, XN = 8, 4

ORDER = [0, 2, 6, 3, 5, 1, 7, 4]
POS = {dz: at for at, dz in enumerate(ORDER)}
BACK = [4, 1, 7, 3, 5, 2, 6, 0]
FAR = [4, 3, 5, 2, 6]

_NAMES = (
    ["pro"]
    + ["px%d" % d for d in range(1, 4)] + ["pz%d" % d for d in range(1, 8)]
    + ["rz%d_%d" % (d, k) for d in (1, 7) for k in range(1, 4)]
    + ["rx%d_%d" % (d, k) for d in range(2, 7) for k in range(1, 4)]
    + ["s%d" % d for d in range(8)] + ["q%d" % d for d in range(8)]
    + ["gx%d_%d" % (d, k) for d in range(2, 7) for k in range(1, 4)]
    + ["gn1", "gn7"] + ["gz%d" % d for d in range(2, 7)] + ["hx%d" % d for d in range(1, 4)]
    + ["y%d_%d_%d" % (s, k, h) for s in range(4) for k in range(4) for h in range(2)]
    + ["out%d" % s for s in range(4)]
)
RS = {name: at for at, name in enumerate(_NAMES)}


def wrap(v, n):
    return lax.rem(v + n, n)


def select(i, values):
    out = (i == 0).astype(jnp.int32) * values[0]
    for at in range(1, len(values)):
        out = out + (i == at).astype(jnp.int32) * values[at]
    return out


def split(v):
    hi = v.astype(BF16)
    return hi, (v - hi.astype(F32)).astype(BF16)


def view(ref, index):
    return lambda: ref.at[index]


def dot(a, b):
    return jnp.dot(a, b, preferred_element_type=F32)


def kernel(
    feat, proto, counts, fg, pg_out,
    cnt, u, ut, utw, ehi, elo, qhi, qlo, ec, ug, sib, cth, ctl, chi, clo, pg, pgo, own,
    tbuf, t1, t2, t3, gxb, gnb, gzb, hxb, y1, y2,
    ssem, rsem, cntsem, t1s, t2s, t3s, t1r, t2r, t3r,
):
    p = lax.axis_index("proto")
    y = lax.axis_index("view")
    c = lax.rem(p, 2)
    x = lax.rem(p // 2, XN)
    z = p // (2 * XN)

    def dev(zz, xx, cc):
        return {"proto": (zz * XN + xx) * 2 + cc}

    sibling = dev(z, x, 1 - c)
    y0, yb1 = lax.rem(y, 2), y // 2
    mate_a = {"view": yb1 * 2 + (1 - y0)}
    mate_b = {"view": (1 - yb1) * 2 + (1 - y0)}
    fbit, gbit = lax.rem(y0 + yb1, 2), yb1

    g8 = lax.rem(p, 8)
    peers = [dict(proto=z * 8 + lax.rem(g8 + k, 8)) for k in range(1, 8)]
    ranks = [lax.rem(g8 + k, 8) for k in range(1, 8)]
    zpeers = [dev(lax.rem(z + k, ZN), x, c) for k in range(1, 8)]
    xpeers = [dev(z, lax.rem(x + k, XN), c) for k in range(1, 4)]

    pro_copy = pltpu.make_async_copy(proto, pg, rsem.at[RS["pro"]])
    pro_copy.start()

    barrier = pltpu.get_barrier_semaphore()
    for d in peers + zpeers + [mate_a, mate_b]:
        pl.semaphore_signal(barrier, inc=1, device_id=d, device_id_type=MESH)

    sent = []

    def send(src, dst, name, device):
        at = len(sent)

        def make():
            return pltpu.make_async_remote_copy(
                src_ref=src() if callable(src) else src, dst_ref=dst() if callable(dst) else dst,
                send_sem=ssem.at[at], recv_sem=rsem.at[RS[name]],
                device_id=device, device_id_type=MESH,
            )

        sent.append(make)
        make().start()

    def arrive(dst, name):
        pltpu.make_async_remote_copy(
            src_ref=dst, dst_ref=dst, send_sem=ssem.at[0], recv_sem=rsem.at[RS[name]],
            device_id=sibling, device_id_type=MESH,
        ).wait_recv()

    zs = [lax.rem(z + d, ZN) for d in range(8)]
    qs = [zs[d] for d in ORDER]

    def ublk(dz, dx):
        return u.at[pl.ds(pl.multiple_of(zs[dz] * GRP + c * HALF + lax.rem(x + dx, XN) * BLK, 8), BLK)]

    def uhalf(dz, core):
        return u.at[pl.ds(pl.multiple_of(zs[dz] * GRP + core * HALF, 8), HALF)]

    blk = {(dz, dx): ublk(dz, dx) for dz in range(8) for dx in range(4)}
    mine_of = [uhalf(dz, c) for dz in range(8)]
    theirs_of = [uhalf(dz, 1 - c) for dz in range(8)]
    own_at = pl.multiple_of(zs[0] * GRP + c * HALF + x * BLK, 8)
    vb = BLK // 2 * 16

    def count_copies(i):
        slot = lax.rem(i, 3)
        copies = []
        group = select(i, qs)
        for b in range(8):
            owner = group * 8 + (b % 4) * 2 + b // 4
            copies.append(
                pltpu.make_async_copy(
                    counts.at[pl.ds(pl.multiple_of(owner * vb, vb), vb)],
                    cnt.at[slot, pl.ds(b * vb, vb)],
                    cntsem.at[slot],
                )
            )
        return copies

    def fetch(i, carry):
        for copy in count_copies(i):
            copy.start()
        return carry

    lax.fori_loop(0, 2, fetch, 0)

    def load_features():
        crops = []
        for j in range(2):
            crops.append(jnp.concatenate([feat[pl.ds(kt * 2 + j, BLK // 2, stride=4), :] for kt in range(2)], axis=1))
        f = jnp.concatenate(crops, axis=0)
        norm = jnp.sqrt(jnp.sum(f * f, axis=1, keepdims=True) + 1e-6)
        return f, norm

    f, norm = load_features()
    u[pl.ds(own_at, BLK), :] = f / norm

    pl.semaphore_wait(barrier, 16)

    own_blk = blk[0, 0]
    for d in (1, 3, 2):
        send(own_blk, own_blk, "px%d" % d, xpeers[d - 1])
    for d in (2, 6, 3, 5, 4, 1, 7):
        send(own_blk, own_blk, "pz%d" % d, zpeers[d - 1])

    pro_copy.wait()

    def centroids(i, carry):
        at = pl.multiple_of(i * 256, 256)
        v = pg[pl.ds(at, 256), :]
        v = v / jnp.sqrt(jnp.sum(v * v, axis=1, keepdims=True) + 1e-6)
        hi, lo = split(v)
        chi[pl.ds(at, 256), :] = hi
        clo[pl.ds(at, 256), :] = lo
        hi, lo = split(jnp.transpose(v * SCORE_SCALE))
        cth[:, pl.ds(at, 256)] = hi
        ctl[:, pl.ds(at, 256)] = lo
        return carry

    lax.fori_loop(0, KL // 256, centroids, 0)
    tbuf[...] = jnp.zeros_like(tbuf)
    eye = lax.broadcasted_iota(jnp.int32, (128, 128), 0) == lax.broadcasted_iota(jnp.int32, (128, 128), 1)

    def to_rows(col, at, first):
        for k in range(3):
            row = jnp.sum(jnp.where(eye, col[k * 128 : (k + 1) * 128], 0.0), axis=0, keepdims=True)
            tbuf[at, first + k : first + k + 1, :] = row

    def relay_z():
        for d in (1, 2, 3):
            arrive(blk[0, 4 - d], "px%d" % d)
        for d in (1, 2, 3):
            send(blk[0, d], blk[0, d], "rz1_%d" % d, zpeers[0])
            send(blk[0, d], blk[0, d], "rz7_%d" % d, zpeers[6])
        send(mine_of[0], mine_of[0], "s0", sibling)

    def relay_x(dz):
        b = blk[dz, 0]
        arrive(b, "pz%d" % (8 - dz))
        for d in (1, 3, 2):
            send(b, b, "rx%d_%d" % (dz, d), xpeers[d - 1])

    def collect(dz):
        if dz in (1, 7):
            arrive(blk[dz, 0], "pz%d" % (8 - dz))
            for d in (1, 2, 3):
                arrive(blk[dz, d], "rz%d_%d" % (8 - dz, d))
        else:
            for d in (1, 2, 3):
                arrive(blk[dz, 4 - d], "rx%d_%d" % (dz, d))
        send(mine_of[dz], mine_of[dz], "s%d" % dz, sibling)

    def use(dz):
        arrive(theirs_of[dz], "s%d" % dz)

    def early_comm(i):
        if i == 2:
            relay_z()
        elif i == 4:
            relay_x(6), relay_x(2)
        elif i == 6:
            relay_x(5), relay_x(3)
        elif i == 7:
            relay_x(4)

    def gather_comm(i):
        if i < 7:
            collect(ORDER[i + 1])
        use(ORDER[i])

    def codes(i, carry):
        for k in range(8):
            @pl.when(i == k)
            def _(k=k):
                early_comm(k)

        slot = lax.rem(i, 3)
        pltpu.make_async_copy(cnt.at[slot], cnt.at[slot], cntsem.at[slot]).wait()

        @pl.when(i < 6)
        def _():
            fetch(i + 2, 0)

        at = pl.multiple_of(i * GRP, GRP)
        sums = []
        for b in range(8):
            rng = pl.ds(pl.multiple_of(at + b * BLK, 16), BLK)
            mass = None
            for kt in range(8):
                v = jnp.concatenate(
                    [cnt[slot, pl.ds(b * vb + kt * 2 + 1 - j, BLK // 2, stride=16), :] for j in range(2)], axis=0
                ).astype(F32)
                mass = v if mass is None else mass + v
                hi, lo = split(v)
                cols = pl.ds(kt * 128, 128)
                qhi[rng, cols] = hi
                qlo[rng, cols] = lo
            sums.append(mass)
        to_rows(jnp.sum(jnp.concatenate(sums, axis=0), axis=1, keepdims=True), select(i, qs), 3)
        rng = pl.ds(at, GRP)
        hi, lo = qhi[rng, :], qlo[rng, :]
        ug[rng, :] = dot(hi, chi[...]) + dot(hi, clo[...]) + dot(lo, chi[...])
        return carry

    def forward(i, carry):
        for k in range(8):
            @pl.when(i == k)
            def _(k=k):
                gather_comm(k)

        group = select(i, qs)
        v = u[pl.ds(pl.multiple_of(group * GRP, 8), GRP), :]
        hi, lo = split(v)
        at = pl.multiple_of(i * GRP, GRP)
        part = None
        for n in range(4):
            cols = pl.ds(n * 256, 256)
            s = dot(hi, cth[:, cols]) + dot(lo, cth[:, cols]) + dot(hi, ctl[:, cols])
            ex = jnp.exp2(s)
            hi_e, lo_e = split(ex)
            ehi[pl.ds(at, GRP), cols] = hi_e
            elo[pl.ds(at, GRP), cols] = lo_e
            two = ex[:, :128] + ex[:, 128:]
            part = two if part is None else part + two
        total = jnp.sum(part, axis=1, keepdims=True)
        hi, lo = split(jnp.transpose(v))
        ut[0:D, pl.ds(at, GRP)] = hi
        ut[D : 2 * D, pl.ds(at, GRP)] = lo
        to_rows(total, group, 0)
        return carry

    lax.fori_loop(0, 8, codes, 0)
    lax.fori_loop(0, 8, forward, 0)

    def small(src, dst, ss, rr, device):
        return pltpu.make_async_remote_copy(
            src_ref=src, dst_ref=dst, send_sem=ss, recv_sem=rr, device_id=device, device_id_type=MESH
        )

    def codes_slab(s):
        cols = pl.ds(s * 256, 256)
        both = dot(ut[...], qhi[:, cols])
        acc = both[:D] + both[D:] + dot(ut[0:D, :], qlo[:, cols])
        pg[cols, :] = jnp.transpose(acc) * (-FIXED_POINT * WEIGHT)

    def forward_grad(i, carry):
        rng = pl.ds(pl.multiple_of(i * GRP, GRP), GRP)
        hi, lo = ehi[rng, :], elo[rng, :]
        ec[rng, :] = dot(hi, chi[...]) + dot(hi, clo[...]) + dot(lo, chi[...])
        return carry

    first = [small(tbuf.at[ranks[k]], t1.at[k], t1s.at[k], t1r.at[k], peers[k]) for k in range(7)]
    for copy in first:
        copy.start()
    codes_slab(0)
    codes_slab(1)
    for copy in first:
        copy.wait()
    mine = tbuf[g8]
    for k in range(7):
        mine = mine + t1[k]
    t2[7] = mine
    second = [small(t2.at[7], t2.at[k], t2s.at[k], t2r.at[k], zpeers[k]) for k in range(7)]
    for copy in second:
        copy.start()
    codes_slab(2)
    codes_slab(3)
    lax.fori_loop(0, 2, forward_grad, 0)
    for copy in second:
        copy.wait()
    mine = t2[7]
    for k in range(7):
        mine = mine + t2[k]
    t3[g8, 0:3, :] = mine[3:6, :] * (FIXED_POINT * WEIGHT) / mine[0:3, :]
    third = [small(t3.at[g8], t3.at[g8], t3s.at[k], t3r.at[k], peers[k]) for k in range(7)]
    for copy in third:
        copy.start()
    lax.fori_loop(2, 8, forward_grad, 0)
    for k in range(7):
        small(t3.at[ranks[6 - k]], t3.at[ranks[6 - k]], t3s.at[k], t3r.at[k], peers[k]).wait_recv()
    for copy in third:
        copy.wait_send()

    def ypart(s):
        h1, h2 = s * 256, s * 256 + 128

        def ds(at, n):
            return pl.ds(pl.multiple_of(at, 8), n)

        return dict(
            away1=(ds(h1 + (1 - fbit) * 64, 64), ds(h2 + (1 - gbit) * 64, 64)),
            keep1=(ds(h1 + fbit * 64, 64), ds(h2 + gbit * 64, 64)),
            away2=(ds(h1 + fbit * 64 + (1 - gbit) * 32, 32), ds(h2 + gbit * 64 + (1 - fbit) * 32, 32)),
            keep2=(ds(h1 + fbit * 64 + gbit * 32, 32), ds(h2 + gbit * 64 + fbit * 32, 32)),
        )

    yparts = [ypart(s) for s in range(4)]

    def out_copy(s):
        rng = pl.ds(s * 256, 256)
        return pltpu.make_async_copy(pgo.at[rng], pg_out.at[rng], rsem.at[RS["out%d" % s]])

    def ystep(k, s):
        part = yparts[s]
        for h in range(2):
            near, far = (mate_a, mate_b) if h == 0 else (mate_b, mate_a)
            name = "y%d_%d_%d" % (s, k - 1, h)
            prev = "y%d_%d_%d" % (s, k - 2, h)
            if k == 1:
                send(view(pg, (part["away1"][h],)), view(y1, (s, h,)), name, near)
            elif k == 2:
                arrive(y1.at[s, h], prev)
                keep = part["keep1"][h]
                pg[keep, :] = pg[keep, :] + y1[s, h]
                send(view(pg, (part["away2"][h],)), view(y2, (s, h,)), name, far)
            elif k == 3:
                arrive(y2.at[s, h], prev)
                keep = part["keep2"][h]
                pgo[keep, :] = pg[keep, :] + y2[s, h]
                send(view(pgo, (keep,)), view(pgo, (keep,)), name, far)
            elif k == 4:
                arrive(pgo.at[part["away2"][h]], prev)
                send(view(pgo, (part["keep1"][h],)), view(pgo, (part["keep1"][h],)), name, near)
            elif k == 5:
                arrive(pgo.at[part["away1"][h]], prev)
        if k == 5:
            out_copy(s).start()

    def slab(s, carry):
        col = pl.multiple_of(s * 256, 256)

        cols = pl.ds(col, 256)
        both = dot(utw[...], ehi[:, cols])
        acc = both[:D] + both[D:] + dot(utw[0:D, :], elo[:, cols])
        pg[cols, :] = jnp.transpose(acc) + pg[cols, :]
        for k in range(4):
            @pl.when(s == k)
            def _(k=k):
                slab_comm(k)
        return carry

    mine_at = [pl.ds(pl.multiple_of(POS[dz] * GRP + c * HALF, 8), HALF) for dz in range(8)]
    theirs_at = [pl.ds(pl.multiple_of(POS[dz] * GRP + (1 - c) * HALF, 8), HALF) for dz in range(8)]

    def gblk(dz, dx):
        return pl.ds(pl.multiple_of(POS[dz] * GRP + c * HALF + lax.rem(x + dx, XN) * BLK, 8), BLK)

    gb = {(dz, dx): gblk(dz, dx) for dz in range(8) for dx in range(4)}

    def from_sibling(dz):
        arrive(sib.at[dz], "q%d" % dz)
        ug[mine_at[dz], :] = ug[mine_at[dz], :] + sib[dz]

    def sums_out(dz):
        from_sibling(dz)
        if dz in (1, 7):
            send(view(ug, (mine_at[dz],)), view(gnb, (dz // 7,)), "gn%d" % dz, zpeers[dz - 1])
        else:
            for d in (2, 1, 3):
                send(view(ug, (gb[dz, d],)), view(gxb, ((dz - 2) * 3 + d - 1,)), "gx%d_%d" % (dz, d), xpeers[d - 1])

    def sums_onward(dz):
        total = ug[gb[dz, 0], :]
        for d in (1, 2, 3):
            arrive(gxb.at[(dz - 2) * 3 + d - 1], "gx%d_%d" % (dz, d))
            total = total + gxb[(dz - 2) * 3 + d - 1]
        ug[gb[dz, 0], :] = total
        send(view(ug, (gb[dz, 0],)), view(gzb, (dz - 2,)), "gz%d" % dz, zpeers[dz - 1])

    def sums_here():
        from_sibling(0)
        for k, dz in enumerate((1, 7)):
            arrive(gnb.at[k], "gn%d" % dz)
        ug[mine_at[0], :] = ug[mine_at[0], :] + gnb[0] + gnb[1]
        for d in (2, 1, 3):
            send(view(ug, (gb[0, d],)), view(hxb, (d - 1,)), "hx%d" % d, xpeers[d - 1])

    def sums_end():
        total = ug[gb[0, 0], :]
        for d in (1, 2, 3):
            arrive(hxb.at[d - 1], "hx%d" % d)
            total = total + hxb[d - 1]
        for d in (2, 6, 3, 5, 4):
            arrive(gzb.at[d - 2], "gz%d" % d)
            total = total + gzb[d - 2]
        own[...] = total

    def slab_comm(k):
        ystep(1, k)
        if k >= 2:
            ystep(2, k - 2)

    def column(group):
        cols = []
        for k in range(3):
            cols.append(jnp.sum(jnp.where(eye, t3[group, k : k + 1, :], 0.0), axis=1, keepdims=True))
        return jnp.concatenate(cols, axis=0)

    def backward(i, carry):
        rng = pl.ds(pl.multiple_of(select(i, back) * GRP, GRP), GRP)
        w = jnp.broadcast_to(column(select(i, backq)), (GRP, D))
        ug[rng, :] = w * ec[rng, :] - ug[rng, :] * (FIXED_POINT * WEIGHT)
        for k in range(8):
            @pl.when(i == k)
            def _(k=k):
                dz = BACK[k]
                send(view(ug, (theirs_at[dz],)), view(sib, (dz,)), "q%d" % dz, sibling)
        return carry

    def weighted(i, carry):
        group = select(i, qs)
        for k in range(3):
            cols = pl.ds(pl.multiple_of(i * GRP + k * 128, 128), 128)
            v = (ut[0:D, cols].astype(F32) + ut[D : 2 * D, cols].astype(F32)) * t3[group, k : k + 1, :]
            hi, lo = split(v)
            utw[0:D, cols] = hi
            utw[D : 2 * D, cols] = lo
        return carry

    back = [POS[dz] for dz in BACK]
    backq = [zs[dz] for dz in BACK]
    lax.fori_loop(0, 8, backward, 0)
    lax.fori_loop(0, 8, weighted, 0)
    for dz in BACK[:7]:
        sums_out(dz)
    lax.fori_loop(0, 4, slab, 0)

    ystep(2, 2)
    ystep(3, 0)
    sums_here()
    for dz in FAR[:3]:
        sums_onward(dz)
    ystep(2, 3)
    ystep(3, 1)
    for dz in FAR[3:]:
        sums_onward(dz)
    ystep(3, 2)
    ystep(4, 0)
    ystep(3, 3)
    ystep(4, 1)
    ystep(4, 2)
    ystep(5, 0)
    sums_end()

    f, norm = load_features()
    unit = f / norm
    grad = own[...]
    inner = jnp.sum(unit * grad, axis=1, keepdims=True)
    out = (grad - unit * inner) / norm
    for j in range(2):
        for kt in range(2):
            piece = out[j * (BLK // 2) : (j + 1) * (BLK // 2), kt * 128 : (kt + 1) * 128]
            fg[pl.ds(kt * 2 + j, BLK // 2, stride=4), :] = piece

    ystep(4, 3)
    ystep(5, 1)
    ystep(5, 2)
    ystep(5, 3)
    for make in sent:
        make().wait_send()
    for s in range(4):
        out_copy(s).wait()


def hand_over(fg, pg, fg_out, pg_out):
    fg_out[...] = fg[...]
    pg_out[...] = pg[...]


def per_device(features, prototypes, code_counts):
    feat = features.reshape(24, 2, 2, 128).transpose(0, 2, 1, 3).reshape(96, 128)
    counts = code_counts.reshape(1536, 2, 8, 128).transpose(0, 2, 1, 3).reshape(1536 * 16, 128)
    vmem, hbm = pl.BlockSpec(memory_space=pltpu.VMEM), pl.BlockSpec(memory_space=pl.ANY)
    dma = pltpu.SemaphoreType.DMA
    fg, pg = pl.pallas_call(
        kernel,
        out_shape=(jax.ShapeDtypeStruct((96, 128), F32), jax.ShapeDtypeStruct((KL, D), F32)),
        in_specs=[vmem, hbm, hbm],
        out_specs=(vmem, hbm),
        scratch_shapes=[
            pltpu.VMEM((3, 8 * BLK // 2 * 16, 128), jnp.int32),
            pltpu.VMEM((ROWS, D), F32),
            pltpu.VMEM((2 * D, ROWS), BF16),
            pltpu.VMEM((2 * D, ROWS), BF16),
            pltpu.VMEM((ROWS, KL), BF16),
            pltpu.VMEM((ROWS, KL), BF16),
            pltpu.VMEM((ROWS, KL), BF16),
            pltpu.VMEM((ROWS, KL), BF16),
            pltpu.VMEM((ROWS, D), F32),
            pltpu.VMEM((ROWS, D), F32),
            pltpu.VMEM((8, HALF, D), F32),
            pltpu.VMEM((D, KL), BF16),
            pltpu.VMEM((D, KL), BF16),
            pltpu.VMEM((KL, D), BF16),
            pltpu.VMEM((KL, D), BF16),
            pltpu.VMEM((KL, D), F32),
            pltpu.VMEM((KL, D), F32),
            pltpu.VMEM((BLK, D), F32),
            pltpu.VMEM((8, 8, 128), F32),
            pltpu.VMEM((7, 8, 128), F32),
            pltpu.VMEM((8, 8, 128), F32),
            pltpu.VMEM((8, 8, 128), F32),
            pltpu.VMEM((15, BLK, D), F32),
            pltpu.VMEM((2, HALF, D), F32),
            pltpu.VMEM((5, BLK, D), F32),
            pltpu.VMEM((3, BLK, D), F32),
            pltpu.VMEM((4, 2, 64, D), F32),
            pltpu.VMEM((4, 2, 32, D), F32),
            dma((128,)),
            dma((len(RS),)),
            dma((3,)),
            dma((7,)), dma((7,)), dma((7,)), dma((7,)), dma((7,)), dma((7,)),
        ],
        compiler_params=pltpu.CompilerParams(
            collective_id=0, has_side_effects=True, vmem_limit_bytes=60 << 20
        ),
        cost_estimate=pl.CostEstimate(flops=18 * ROWS * KL * D, bytes_accessed=16 << 20, transcendentals=ROWS * KL),
    )(feat, prototypes, counts)
    fg, pg = pl.pallas_call(
        hand_over,
        out_shape=(jax.ShapeDtypeStruct((96, 128), F32), jax.ShapeDtypeStruct((KL, D), F32)),
        in_specs=[vmem, vmem],
        out_specs=(vmem, vmem),
    )(fg, pg)
    features_grad = fg.reshape(24, 2, 2, 128).transpose(0, 2, 1, 3).reshape(24, 2, 256)
    return features_grad, pg


def solution(mesh):
    in_specs = (P(("view", "proto"), None, None), P("proto", None), P("view", None, "proto"))
    out_specs = (P(("view", "proto"), None, None), P("proto", None))
    return jax.shard_map(
        per_device, mesh=mesh, in_specs=in_specs, out_specs=out_specs, check_vma=False
    )
```

```python
import jax
import jax.numpy as jnp
from jax import lax
from jax.experimental import pallas as pl
from jax.experimental.pallas import tpu as pltpu
from jax.sharding import PartitionSpec as P

MESH = pl.DeviceIdType.MESH
F32 = jnp.float32
BF16 = jnp.bfloat16
WEIGHT = 4096.0 / 0.1
FIXED_POINT = 2.0 ** (-24)
SCORE_SCALE = 10.0 * 1.4426950408889634

D = 256
KL = 1024
BLK = 48
HALF = 4 * BLK
GRP = 2 * HALF
ROWS = 8 * GRP
ZN, XN = 8, 4

ORDER = [0, 2, 6, 3, 5, 1, 7, 4]
POS = {dz: at for at, dz in enumerate(ORDER)}
BACK = [4, 1, 7, 3, 5, 2, 6, 0]
FAR = [4, 3, 5, 2, 6]

_NAMES = (
    ["pro"]
    + ["px%d" % d for d in range(1, 4)] + ["pz%d" % d for d in range(1, 8)]
    + ["rz%d_%d" % (d, k) for d in (1, 7) for k in range(1, 4)]
    + ["rx%d_%d" % (d, k) for d in range(2, 7) for k in range(1, 4)]
    + ["s%d" % d for d in range(8)] + ["q%d" % d for d in range(8)]
    + ["gx%d_%d" % (d, k) for d in range(2, 7) for k in range(1, 4)]
    + ["gn1", "gn7"] + ["gz%d" % d for d in range(2, 7)] + ["hx%d" % d for d in range(1, 4)]
    + ["y%d_%d_%d" % (s, k, h) for s in range(4) for k in range(4) for h in range(2)]
    + ["out%d" % s for s in range(4)]
)
RS = {name: at for at, name in enumerate(_NAMES)}


def wrap(v, n):
    return lax.rem(v + n, n)


def select(i, values):
    out = (i == 0).astype(jnp.int32) * values[0]
    for at in range(1, len(values)):
        out = out + (i == at).astype(jnp.int32) * values[at]
    return out


def split(v):
    hi = v.astype(BF16)
    return hi, (v - hi.astype(F32)).astype(BF16)


def view(ref, index):
    return lambda: ref.at[index]


def dot(a, b):
    return jnp.dot(a, b, preferred_element_type=F32)


def kernel(
    feat, proto, counts, fg, pg_out,
    cnt, u, ut, utw, ehi, elo, qhi, qlo, ec, ug, sib, cth, ctl, chi, clo, pg, pgo, own,
    tbuf, t1, t2, t3, gxb, gnb, gzb, hxb, y1, y2,
    ssem, rsem, cntsem, t1s, t2s, t3s, t1r, t2r, t3r,
):
    p = lax.axis_index("proto")
    y = lax.axis_index("view")
    c = lax.rem(p, 2)
    x = lax.rem(p // 2, XN)
    z = p // (2 * XN)

    def dev(zz, xx, cc):
        return {"proto": (zz * XN + xx) * 2 + cc}

    sibling = dev(z, x, 1 - c)
    y0, yb1 = lax.rem(y, 2), y // 2
    mate_a = {"view": yb1 * 2 + (1 - y0)}
    mate_b = {"view": (1 - yb1) * 2 + (1 - y0)}
    fbit, gbit = lax.rem(y0 + yb1, 2), yb1

    g8 = lax.rem(p, 8)
    peers = [dict(proto=z * 8 + lax.rem(g8 + k, 8)) for k in range(1, 8)]
    ranks = [lax.rem(g8 + k, 8) for k in range(1, 8)]
    zpeers = [dev(lax.rem(z + k, ZN), x, c) for k in range(1, 8)]
    xpeers = [dev(z, lax.rem(x + k, XN), c) for k in range(1, 4)]

    pro_copy = pltpu.make_async_copy(proto, pg, rsem.at[RS["pro"]])
    pro_copy.start()

    barrier = pltpu.get_barrier_semaphore()
    for d in peers + zpeers + [mate_a, mate_b]:
        pl.semaphore_signal(barrier, inc=1, device_id=d, device_id_type=MESH)

    sent = []

    def send(src, dst, name, device):
        at = len(sent)

        def make():
            return pltpu.make_async_remote_copy(
                src_ref=src() if callable(src) else src, dst_ref=dst() if callable(dst) else dst,
                send_sem=ssem.at[at], recv_sem=rsem.at[RS[name]],
                device_id=device, device_id_type=MESH,
            )

        sent.append(make)
        make().start()

    def arrive(dst, name):
        pltpu.make_async_remote_copy(
            src_ref=dst, dst_ref=dst, send_sem=ssem.at[0], recv_sem=rsem.at[RS[name]],
            device_id=sibling, device_id_type=MESH,
        ).wait_recv()

    zs = [lax.rem(z + d, ZN) for d in range(8)]
    qs = [zs[d] for d in ORDER]

    def ublk(dz, dx):
        return u.at[pl.ds(pl.multiple_of(zs[dz] * GRP + c * HALF + lax.rem(x + dx, XN) * BLK, 8), BLK)]

    def uhalf(dz, core):
        return u.at[pl.ds(pl.multiple_of(zs[dz] * GRP + core * HALF, 8), HALF)]

    blk = {(dz, dx): ublk(dz, dx) for dz in range(8) for dx in range(4)}
    mine_of = [uhalf(dz, c) for dz in range(8)]
    theirs_of = [uhalf(dz, 1 - c) for dz in range(8)]
    own_at = pl.multiple_of(zs[0] * GRP + c * HALF + x * BLK, 8)
    vb = BLK // 2 * 16

    def count_copies(i):
        slot = lax.rem(i, 3)
        copies = []
        group = select(i, qs)
        for b in range(8):
            owner = group * 8 + (b % 4) * 2 + b // 4
            copies.append(
                pltpu.make_async_copy(
                    counts.at[pl.ds(pl.multiple_of(owner * vb, vb), vb)],
                    cnt.at[slot, pl.ds(b * vb, vb)],
                    cntsem.at[slot],
                )
            )
        return copies

    def fetch(i, carry):
        for copy in count_copies(i):
            copy.start()
        return carry

    lax.fori_loop(0, 2, fetch, 0)

    def load_features():
        crops = []
        for j in range(2):
            crops.append(jnp.concatenate([feat[pl.ds(kt * 2 + j, BLK // 2, stride=4), :] for kt in range(2)], axis=1))
        f = jnp.concatenate(crops, axis=0)
        norm = jnp.sqrt(jnp.sum(f * f, axis=1, keepdims=True) + 1e-6)
        return f, norm

    f, norm = load_features()
    u[pl.ds(own_at, BLK), :] = f / norm

    pl.semaphore_wait(barrier, 16)

    own_blk = blk[0, 0]
    for d in (1, 3, 2):
        send(own_blk, own_blk, "px%d" % d, xpeers[d - 1])
    for d in (2, 6, 3, 5, 4, 1, 7):
        send(own_blk, own_blk, "pz%d" % d, zpeers[d - 1])

    pro_copy.wait()

    def centroids(i, carry):
        at = pl.multiple_of(i * 256, 256)
        v = pg[pl.ds(at, 256), :]
        v = v / jnp.sqrt(jnp.sum(v * v, axis=1, keepdims=True) + 1e-6)
        hi, lo = split(v)
        chi[pl.ds(at, 256), :] = hi
        clo[pl.ds(at, 256), :] = lo
        hi, lo = split(jnp.transpose(v * SCORE_SCALE))
        cth[:, pl.ds(at, 256)] = hi
        ctl[:, pl.ds(at, 256)] = lo
        return carry

    lax.fori_loop(0, KL // 256, centroids, 0)
    tbuf[...] = jnp.zeros_like(tbuf)
    eye = lax.broadcasted_iota(jnp.int32, (128, 128), 0) == lax.broadcasted_iota(jnp.int32, (128, 128), 1)

    def to_rows(col, at, first):
        for k in range(3):
            row = jnp.sum(jnp.where(eye, col[k * 128 : (k + 1) * 128], 0.0), axis=0, keepdims=True)
            tbuf[at, first + k : first + k + 1, :] = row

    def relay_z():
        for d in (1, 2, 3):
            arrive(blk[0, 4 - d], "px%d" % d)
        for d in (1, 2, 3):
            send(blk[0, d], blk[0, d], "rz1_%d" % d, zpeers[0])
            send(blk[0, d], blk[0, d], "rz7_%d" % d, zpeers[6])
        send(mine_of[0], mine_of[0], "s0", sibling)

    def relay_x(dz):
        b = blk[dz, 0]
        arrive(b, "pz%d" % (8 - dz))
        for d in (1, 3, 2):
            send(b, b, "rx%d_%d" % (dz, d), xpeers[d - 1])

    def collect(dz):
        if dz in (1, 7):
            arrive(blk[dz, 0], "pz%d" % (8 - dz))
            for d in (1, 2, 3):
                arrive(blk[dz, d], "rz%d_%d" % (8 - dz, d))
        else:
            for d in (1, 2, 3):
                arrive(blk[dz, 4 - d], "rx%d_%d" % (dz, d))
        send(mine_of[dz], mine_of[dz], "s%d" % dz, sibling)

    def use(dz):
        arrive(theirs_of[dz], "s%d" % dz)

    def early_comm(i):
        if i == 2:
            relay_z()
        elif i == 4:
            relay_x(6), relay_x(2)
        elif i == 6:
            relay_x(5), relay_x(3)
        elif i == 7:
            relay_x(4)

    def gather_comm(i):
        if i < 7:
            collect(ORDER[i + 1])
        use(ORDER[i])

    def codes(i, carry):
        for k in range(8):
            @pl.when(i == k)
            def _(k=k):
                early_comm(k)

        slot = lax.rem(i, 3)
        pltpu.make_async_copy(cnt.at[slot], cnt.at[slot], cntsem.at[slot]).wait()

        @pl.when(i < 6)
        def _():
            fetch(i + 2, 0)

        at = pl.multiple_of(i * GRP, GRP)
        sums = []
        for b in range(8):
            rng = pl.ds(pl.multiple_of(at + b * BLK, 16), BLK)
            mass = None
            for kt in range(8):
                v = jnp.concatenate(
                    [cnt[slot, pl.ds(b * vb + kt * 2 + 1 - j, BLK // 2, stride=16), :] for j in range(2)], axis=0
                ).astype(F32)
                mass = v if mass is None else mass + v
                hi, lo = split(v)
                cols = pl.ds(kt * 128, 128)
                qhi[rng, cols] = hi
                qlo[rng, cols] = lo
            sums.append(mass)
        to_rows(jnp.sum(jnp.concatenate(sums, axis=0), axis=1, keepdims=True), select(i, qs), 3)
        rng = pl.ds(at, GRP)
        hi, lo = qhi[rng, :], qlo[rng, :]
        ug[rng, :] = dot(hi, chi[...]) + dot(hi, clo[...]) + dot(lo, chi[...])
        return carry

    def forward(i, carry):
        for k in range(8):
            @pl.when(i == k)
            def _(k=k):
                gather_comm(k)

        group = select(i, qs)
        v = u[pl.ds(pl.multiple_of(group * GRP, 8), GRP), :]
        hi, lo = split(v)
        at = pl.multiple_of(i * GRP, GRP)
        part = None
        for n in range(4):
            cols = pl.ds(n * 256, 256)
            s = dot(hi, cth[:, cols]) + dot(lo, cth[:, cols]) + dot(hi, ctl[:, cols])
            ex = jnp.exp2(s)
            hi_e, lo_e = split(ex)
            ehi[pl.ds(at, GRP), cols] = hi_e
            elo[pl.ds(at, GRP), cols] = lo_e
            two = ex[:, :128] + ex[:, 128:]
            part = two if part is None else part + two
        total = jnp.sum(part, axis=1, keepdims=True)
        hi, lo = split(jnp.transpose(v))
        ut[0:D, pl.ds(at, GRP)] = hi
        ut[D : 2 * D, pl.ds(at, GRP)] = lo
        to_rows(total, group, 0)
        return carry

    lax.fori_loop(0, 8, codes, 0)
    lax.fori_loop(0, 8, forward, 0)

    def small(src, dst, ss, rr, device):
        return pltpu.make_async_remote_copy(
            src_ref=src, dst_ref=dst, send_sem=ss, recv_sem=rr, device_id=device, device_id_type=MESH
        )

    def codes_slab(s):
        cols = pl.ds(s * 256, 256)
        both = dot(ut[...], qhi[:, cols])
        acc = both[:D] + both[D:] + dot(ut[0:D, :], qlo[:, cols])
        pg[cols, :] = jnp.transpose(acc) * (-FIXED_POINT * WEIGHT)

    def forward_grad(i, carry):
        rng = pl.ds(pl.multiple_of(i * GRP, GRP), GRP)
        hi, lo = ehi[rng, :], elo[rng, :]
        ec[rng, :] = dot(hi, chi[...]) + dot(hi, clo[...]) + dot(lo, chi[...])
        return carry

    first = [small(tbuf.at[ranks[k]], t1.at[k], t1s.at[k], t1r.at[k], peers[k]) for k in range(7)]
    for copy in first:
        copy.start()
    codes_slab(0)
    codes_slab(1)
    lax.fori_loop(0, 1, forward_grad, 0)
    for copy in first:
        copy.wait()
    mine = tbuf[g8]
    for k in range(7):
        mine = mine + t1[k]
    t2[7] = mine
    second = [small(t2.at[7], t2.at[k], t2s.at[k], t2r.at[k], zpeers[k]) for k in range(7)]
    for copy in second:
        copy.start()
    codes_slab(2)
    codes_slab(3)
    lax.fori_loop(1, 4, forward_grad, 0)
    for copy in second:
        copy.wait()
    mine = t2[7]
    for k in range(7):
        mine = mine + t2[k]
    t3[g8, 0:3, :] = mine[3:6, :] * (FIXED_POINT * WEIGHT) / mine[0:3, :]
    third = [small(t3.at[g8], t3.at[g8], t3s.at[k], t3r.at[k], peers[k]) for k in range(7)]
    for copy in third:
        copy.start()
    lax.fori_loop(4, 8, forward_grad, 0)
    for k in range(7):
        small(t3.at[ranks[6 - k]], t3.at[ranks[6 - k]], t3s.at[k], t3r.at[k], peers[k]).wait_recv()
    for copy in third:
        copy.wait_send()

    def ypart(s):
        h1, h2 = s * 256, s * 256 + 128

        def ds(at, n):
            return pl.ds(pl.multiple_of(at, 8), n)

        return dict(
            away1=(ds(h1 + (1 - fbit) * 64, 64), ds(h2 + (1 - gbit) * 64, 64)),
            keep1=(ds(h1 + fbit * 64, 64), ds(h2 + gbit * 64, 64)),
            away2=(ds(h1 + fbit * 64 + (1 - gbit) * 32, 32), ds(h2 + gbit * 64 + (1 - fbit) * 32, 32)),
            keep2=(ds(h1 + fbit * 64 + gbit * 32, 32), ds(h2 + gbit * 64 + fbit * 32, 32)),
        )

    yparts = [ypart(s) for s in range(4)]

    def out_copy(s):
        rng = pl.ds(s * 256, 256)
        return pltpu.make_async_copy(pgo.at[rng], pg_out.at[rng], rsem.at[RS["out%d" % s]])

    def ystep(k, s):
        part = yparts[s]
        for h in range(2):
            near, far = (mate_a, mate_b) if h == 0 else (mate_b, mate_a)
            name = "y%d_%d_%d" % (s, k - 1, h)
            prev = "y%d_%d_%d" % (s, k - 2, h)
            if k == 1:
                send(view(pg, (part["away1"][h],)), view(y1, (s, h,)), name, near)
            elif k == 2:
                arrive(y1.at[s, h], prev)
                keep = part["keep1"][h]
                pg[keep, :] = pg[keep, :] + y1[s, h]
                send(view(pg, (part["away2"][h],)), view(y2, (s, h,)), name, far)
            elif k == 3:
                arrive(y2.at[s, h], prev)
                keep = part["keep2"][h]
                pgo[keep, :] = pg[keep, :] + y2[s, h]
                send(view(pgo, (keep,)), view(pgo, (keep,)), name, far)
            elif k == 4:
                arrive(pgo.at[part["away2"][h]], prev)
                send(view(pgo, (part["keep1"][h],)), view(pgo, (part["keep1"][h],)), name, near)
            elif k == 5:
                arrive(pgo.at[part["away1"][h]], prev)
        if k == 5:
            out_copy(s).start()

    def slab(s, carry):
        col = pl.multiple_of(s * 256, 256)

        cols = pl.ds(col, 256)
        both = dot(utw[...], ehi[:, cols])
        acc = both[:D] + both[D:] + dot(utw[0:D, :], elo[:, cols])
        pg[cols, :] = jnp.transpose(acc) + pg[cols, :]
        for k in range(4):
            @pl.when(s == k)
            def _(k=k):
                slab_comm(k)
        return carry

    mine_at = [pl.ds(pl.multiple_of(POS[dz] * GRP + c * HALF, 8), HALF) for dz in range(8)]
    theirs_at = [pl.ds(pl.multiple_of(POS[dz] * GRP + (1 - c) * HALF, 8), HALF) for dz in range(8)]

    def gblk(dz, dx):
        return pl.ds(pl.multiple_of(POS[dz] * GRP + c * HALF + lax.rem(x + dx, XN) * BLK, 8), BLK)

    gb = {(dz, dx): gblk(dz, dx) for dz in range(8) for dx in range(4)}

    def from_sibling(dz):
        arrive(sib.at[dz], "q%d" % dz)
        ug[mine_at[dz], :] = ug[mine_at[dz], :] + sib[dz]

    def sums_out(dz):
        from_sibling(dz)
        if dz in (1, 7):
            send(view(ug, (mine_at[dz],)), view(gnb, (dz // 7,)), "gn%d" % dz, zpeers[dz - 1])
        else:
            for d in (2, 1, 3):
                send(view(ug, (gb[dz, d],)), view(gxb, ((dz - 2) * 3 + d - 1,)), "gx%d_%d" % (dz, d), xpeers[d - 1])

    def sums_onward(dz):
        total = ug[gb[dz, 0], :]
        for d in (1, 2, 3):
            arrive(gxb.at[(dz - 2) * 3 + d - 1], "gx%d_%d" % (dz, d))
            total = total + gxb[(dz - 2) * 3 + d - 1]
        ug[gb[dz, 0], :] = total
        send(view(ug, (gb[dz, 0],)), view(gzb, (dz - 2,)), "gz%d" % dz, zpeers[dz - 1])

    def sums_here():
        from_sibling(0)
        for k, dz in enumerate((1, 7)):
            arrive(gnb.at[k], "gn%d" % dz)
        ug[mine_at[0], :] = ug[mine_at[0], :] + gnb[0] + gnb[1]
        for d in (2, 1, 3):
            send(view(ug, (gb[0, d],)), view(hxb, (d - 1,)), "hx%d" % d, xpeers[d - 1])

    def sums_end():
        total = ug[gb[0, 0], :]
        for d in (1, 2, 3):
            arrive(hxb.at[d - 1], "hx%d" % d)
            total = total + hxb[d - 1]
        for d in (2, 6, 3, 5, 4):
            arrive(gzb.at[d - 2], "gz%d" % d)
            total = total + gzb[d - 2]
        own[...] = total

    def slab_comm(k):
        ystep(1, k)
        if k >= 2:
            ystep(2, k - 2)

    def column(group):
        cols = []
        for k in range(3):
            cols.append(jnp.sum(jnp.where(eye, t3[group, k : k + 1, :], 0.0), axis=1, keepdims=True))
        return jnp.concatenate(cols, axis=0)

    def backward(i, carry):
        rng = pl.ds(pl.multiple_of(select(i, back) * GRP, GRP), GRP)
        w = jnp.broadcast_to(column(select(i, backq)), (GRP, D))
        ug[rng, :] = w * ec[rng, :] - ug[rng, :] * (FIXED_POINT * WEIGHT)
        for k in range(8):
            @pl.when(i == k)
            def _(k=k):
                dz = BACK[k]
                send(view(ug, (theirs_at[dz],)), view(sib, (dz,)), "q%d" % dz, sibling)
        return carry

    def weighted(i, carry):
        group = select(i, qs)
        for k in range(3):
            cols = pl.ds(pl.multiple_of(i * GRP + k * 128, 128), 128)
            v = (ut[0:D, cols].astype(F32) + ut[D : 2 * D, cols].astype(F32)) * t3[group, k : k + 1, :]
            hi, lo = split(v)
            utw[0:D, cols] = hi
            utw[D : 2 * D, cols] = lo
        return carry

    back = [POS[dz] for dz in BACK]
    backq = [zs[dz] for dz in BACK]
    lax.fori_loop(0, 8, backward, 0)
    lax.fori_loop(0, 8, weighted, 0)
    for dz in BACK[:7]:
        sums_out(dz)
    lax.fori_loop(0, 4, slab, 0)

    ystep(2, 2)
    ystep(3, 0)
    sums_here()
    for dz in FAR[:3]:
        sums_onward(dz)
    ystep(2, 3)
    ystep(3, 1)
    for dz in FAR[3:]:
        sums_onward(dz)
    ystep(3, 2)
    ystep(4, 0)
    ystep(3, 3)
    ystep(4, 1)
    ystep(4, 2)
    ystep(5, 0)
    sums_end()

    f, norm = load_features()
    unit = f / norm
    grad = own[...]
    inner = jnp.sum(unit * grad, axis=1, keepdims=True)
    out = (grad - unit * inner) / norm
    for j in range(2):
        for kt in range(2):
            piece = out[j * (BLK // 2) : (j + 1) * (BLK // 2), kt * 128 : (kt + 1) * 128]
            fg[pl.ds(kt * 2 + j, BLK // 2, stride=4), :] = piece

    ystep(4, 3)
    ystep(5, 1)
    ystep(5, 2)
    ystep(5, 3)
    for make in sent:
        make().wait_send()
    for s in range(4):
        out_copy(s).wait()


def hand_over(fg, pg, fg_out, pg_out):
    fg_out[...] = fg[...]
    pg_out[...] = pg[...]


def per_device(features, prototypes, code_counts):
    feat = features.reshape(24, 2, 2, 128).transpose(0, 2, 1, 3).reshape(96, 128)
    counts = code_counts.reshape(1536, 2, 8, 128).transpose(0, 2, 1, 3).reshape(1536 * 16, 128)
    vmem, hbm = pl.BlockSpec(memory_space=pltpu.VMEM), pl.BlockSpec(memory_space=pl.ANY)
    dma = pltpu.SemaphoreType.DMA
    fg, pg = pl.pallas_call(
        kernel,
        out_shape=(jax.ShapeDtypeStruct((96, 128), F32), jax.ShapeDtypeStruct((KL, D), F32)),
        in_specs=[vmem, hbm, hbm],
        out_specs=(vmem, hbm),
        scratch_shapes=[
            pltpu.VMEM((3, 8 * BLK // 2 * 16, 128), jnp.int32),
            pltpu.VMEM((ROWS, D), F32),
            pltpu.VMEM((2 * D, ROWS), BF16),
            pltpu.VMEM((2 * D, ROWS), BF16),
            pltpu.VMEM((ROWS, KL), BF16),
            pltpu.VMEM((ROWS, KL), BF16),
            pltpu.VMEM((ROWS, KL), BF16),
            pltpu.VMEM((ROWS, KL), BF16),
            pltpu.VMEM((ROWS, D), F32),
            pltpu.VMEM((ROWS, D), F32),
            pltpu.VMEM((8, HALF, D), F32),
            pltpu.VMEM((D, KL), BF16),
            pltpu.VMEM((D, KL), BF16),
            pltpu.VMEM((KL, D), BF16),
            pltpu.VMEM((KL, D), BF16),
            pltpu.VMEM((KL, D), F32),
            pltpu.VMEM((KL, D), F32),
            pltpu.VMEM((BLK, D), F32),
            pltpu.VMEM((8, 8, 128), F32),
            pltpu.VMEM((7, 8, 128), F32),
            pltpu.VMEM((8, 8, 128), F32),
            pltpu.VMEM((8, 8, 128), F32),
            pltpu.VMEM((15, BLK, D), F32),
            pltpu.VMEM((2, HALF, D), F32),
            pltpu.VMEM((5, BLK, D), F32),
            pltpu.VMEM((3, BLK, D), F32),
            pltpu.VMEM((4, 2, 64, D), F32),
            pltpu.VMEM((4, 2, 32, D), F32),
            dma((128,)),
            dma((len(RS),)),
            dma((3,)),
            dma((7,)), dma((7,)), dma((7,)), dma((7,)), dma((7,)), dma((7,)),
        ],
        compiler_params=pltpu.CompilerParams(
            collective_id=0, has_side_effects=True, vmem_limit_bytes=60 << 20
        ),
        cost_estimate=pl.CostEstimate(flops=18 * ROWS * KL * D, bytes_accessed=16 << 20, transcendentals=ROWS * KL),
    )(feat, prototypes, counts)
    fg, pg = pl.pallas_call(
        hand_over,
        out_shape=(jax.ShapeDtypeStruct((96, 128), F32), jax.ShapeDtypeStruct((KL, D), F32)),
        in_specs=[vmem, vmem],
        out_specs=(vmem, vmem),
    )(fg, pg)
    features_grad = fg.reshape(24, 2, 2, 128).transpose(0, 2, 1, 3).reshape(24, 2, 256)
    return features_grad, pg


def solution(mesh):
    in_specs = (P(("view", "proto"), None, None), P("proto", None), P("view", None, "proto"))
    out_specs = (P(("view", "proto"), None, None), P("proto", None))
    return jax.shard_map(
        per_device, mesh=mesh, in_specs=in_specs, out_specs=out_specs, check_vma=False
    )
```

```python
import jax
import jax.numpy as jnp
from jax import lax
from jax.experimental import pallas as pl
from jax.experimental.pallas import tpu as pltpu
from jax.sharding import PartitionSpec as P

MESH = pl.DeviceIdType.MESH
F32 = jnp.float32
BF16 = jnp.bfloat16
WEIGHT = 4096.0 / 0.1
FIXED_POINT = 2.0 ** (-24)
SCORE_SCALE = 10.0 * 1.4426950408889634

D = 256
KL = 1024
BLK = 48
HALF = 4 * BLK
GRP = 2 * HALF
ROWS = 8 * GRP
ZN, XN = 8, 4

ORDER = [0, 2, 6, 3, 5, 1, 7, 4]
POS = {dz: at for at, dz in enumerate(ORDER)}
BACK = [4, 1, 7, 3, 5, 2, 6, 0]
FAR = [4, 3, 5, 2, 6]

_NAMES = (
    ["pro"]
    + ["px%d" % d for d in range(1, 4)] + ["pz%d" % d for d in range(1, 8)]
    + ["rz%d_%d" % (d, k) for d in (1, 7) for k in range(1, 4)]
    + ["rx%d_%d" % (d, k) for d in range(2, 7) for k in range(1, 4)]
    + ["s%d" % d for d in range(8)] + ["q%d" % d for d in range(8)]
    + ["gx%d_%d" % (d, k) for d in range(2, 7) for k in range(1, 4)]
    + ["gn1", "gn7"] + ["gz%d" % d for d in range(2, 7)] + ["hx%d" % d for d in range(1, 4)]
    + ["y%d_%d_%d" % (s, k, h) for s in range(4) for k in range(4) for h in range(2)]
    + ["out%d" % s for s in range(4)]
)
RS = {name: at for at, name in enumerate(_NAMES)}


def wrap(v, n):
    return lax.rem(v + n, n)


def select(i, values):
    out = (i == 0).astype(jnp.int32) * values[0]
    for at in range(1, len(values)):
        out = out + (i == at).astype(jnp.int32) * values[at]
    return out


def split(v):
    hi = v.astype(BF16)
    return hi, (v - hi.astype(F32)).astype(BF16)


def view(ref, index):
    return lambda: ref.at[index]


def dot(a, b):
    return jnp.dot(a, b, preferred_element_type=F32)


def kernel(
    feat, proto, counts, fg, pg_out,
    cnt, u, ut, utw, ehi, elo, qhi, qlo, ec, ug, sib, cth, ctl, chi, clo, pg, pgo, own,
    tbuf, t1, t2, t3, gxb, gnb, gzb, hxb, y1, y2,
    ssem, rsem, cntsem, t1s, t2s, t3s, t1r, t2r, t3r,
):
    p = lax.axis_index("proto")
    y = lax.axis_index("view")
    c = lax.rem(p, 2)
    x = lax.rem(p // 2, XN)
    z = p // (2 * XN)

    def dev(zz, xx, cc):
        return {"proto": (zz * XN + xx) * 2 + cc}

    sibling = dev(z, x, 1 - c)
    y0, yb1 = lax.rem(y, 2), y // 2
    mate_a = {"view": yb1 * 2 + (1 - y0)}
    mate_b = {"view": (1 - yb1) * 2 + (1 - y0)}
    fbit, gbit = lax.rem(y0 + yb1, 2), yb1

    g8 = lax.rem(p, 8)
    peers = [dict(proto=z * 8 + lax.rem(g8 + k, 8)) for k in range(1, 8)]
    ranks = [lax.rem(g8 + k, 8) for k in range(1, 8)]
    zpeers = [dev(lax.rem(z + k, ZN), x, c) for k in range(1, 8)]
    xpeers = [dev(z, lax.rem(x + k, XN), c) for k in range(1, 4)]

    pro_copy = pltpu.make_async_copy(proto, pg, rsem.at[RS["pro"]])
    pro_copy.start()

    barrier = pltpu.get_barrier_semaphore()
    for d in peers + zpeers + [mate_a, mate_b]:
        pl.semaphore_signal(barrier, inc=1, device_id=d, device_id_type=MESH)

    sent = []

    def send(src, dst, name, device):
        at = len(sent)

        def make():
            return pltpu.make_async_remote_copy(
                src_ref=src() if callable(src) else src, dst_ref=dst() if callable(dst) else dst,
                send_sem=ssem.at[at], recv_sem=rsem.at[RS[name]],
                device_id=device, device_id_type=MESH,
            )

        sent.append(make)
        make().start()

    def arrive(dst, name):
        pltpu.make_async_remote_copy(
            src_ref=dst, dst_ref=dst, send_sem=ssem.at[0], recv_sem=rsem.at[RS[name]],
            device_id=sibling, device_id_type=MESH,
        ).wait_recv()

    zs = [lax.rem(z + d, ZN) for d in range(8)]
    qs = [zs[d] for d in ORDER]

    def ublk(dz, dx):
        return u.at[pl.ds(pl.multiple_of(zs[dz] * GRP + c * HALF + lax.rem(x + dx, XN) * BLK, 8), BLK)]

    def uhalf(dz, core):
        return u.at[pl.ds(pl.multiple_of(zs[dz] * GRP + core * HALF, 8), HALF)]

    blk = {(dz, dx): ublk(dz, dx) for dz in range(8) for dx in range(4)}
    mine_of = [uhalf(dz, c) for dz in range(8)]
    theirs_of = [uhalf(dz, 1 - c) for dz in range(8)]
    own_at = pl.multiple_of(zs[0] * GRP + c * HALF + x * BLK, 8)
    vb = BLK // 2 * 16

    def count_copies(i):
        slot = lax.rem(i, 3)
        copies = []
        group = select(i, qs)
        for b in range(8):
            owner = group * 8 + (b % 4) * 2 + b // 4
            copies.append(
                pltpu.make_async_copy(
                    counts.at[pl.ds(pl.multiple_of(owner * vb, vb), vb)],
                    cnt.at[slot, pl.ds(b * vb, vb)],
                    cntsem.at[slot],
                )
            )
        return copies

    def fetch(i, carry):
        for copy in count_copies(i):
            copy.start()
        return carry

    lax.fori_loop(0, 2, fetch, 0)

    def load_features():
        crops = []
        for j in range(2):
            crops.append(jnp.concatenate([feat[pl.ds(kt * 2 + j, BLK // 2, stride=4), :] for kt in range(2)], axis=1))
        f = jnp.concatenate(crops, axis=0)
        norm = jnp.sqrt(jnp.sum(f * f, axis=1, keepdims=True) + 1e-6)
        return f, norm

    f, norm = load_features()
    u[pl.ds(own_at, BLK), :] = f / norm

    pl.semaphore_wait(barrier, 16)

    own_blk = blk[0, 0]
    for d in (1, 3, 2):
        send(own_blk, own_blk, "px%d" % d, xpeers[d - 1])
    for d in (2, 6, 3, 5, 4, 1, 7):
        send(own_blk, own_blk, "pz%d" % d, zpeers[d - 1])

    pro_copy.wait()

    def centroids(i, carry):
        at = pl.multiple_of(i * 256, 256)
        v = pg[pl.ds(at, 256), :]
        v = v / jnp.sqrt(jnp.sum(v * v, axis=1, keepdims=True) + 1e-6)
        hi, lo = split(v)
        chi[pl.ds(at, 256), :] = hi
        clo[pl.ds(at, 256), :] = lo
        hi, lo = split(jnp.transpose(v * SCORE_SCALE))
        cth[:, pl.ds(at, 256)] = hi
        ctl[:, pl.ds(at, 256)] = lo
        return carry

    lax.fori_loop(0, KL // 256, centroids, 0)
    tbuf[...] = jnp.zeros_like(tbuf)
    eye = lax.broadcasted_iota(jnp.int32, (128, 128), 0) == lax.broadcasted_iota(jnp.int32, (128, 128), 1)

    def to_rows(col, at, first):
        for k in range(3):
            row = jnp.sum(jnp.where(eye, col[k * 128 : (k + 1) * 128], 0.0), axis=0, keepdims=True)
            tbuf[at, first + k : first + k + 1, :] = row

    def relay_z():
        for d in (1, 2, 3):
            arrive(blk[0, 4 - d], "px%d" % d)
        for d in (1, 2, 3):
            send(blk[0, d], blk[0, d], "rz1_%d" % d, zpeers[0])
            send(blk[0, d], blk[0, d], "rz7_%d" % d, zpeers[6])
        send(mine_of[0], mine_of[0], "s0", sibling)

    def relay_x(dz):
        b = blk[dz, 0]
        arrive(b, "pz%d" % (8 - dz))
        for d in (1, 3, 2):
            send(b, b, "rx%d_%d" % (dz, d), xpeers[d - 1])

    def collect(dz):
        if dz in (1, 7):
            arrive(blk[dz, 0], "pz%d" % (8 - dz))
            for d in (1, 2, 3):
                arrive(blk[dz, d], "rz%d_%d" % (8 - dz, d))
        else:
            for d in (1, 2, 3):
                arrive(blk[dz, 4 - d], "rx%d_%d" % (dz, d))
        send(mine_of[dz], mine_of[dz], "s%d" % dz, sibling)

    def use(dz):
        arrive(theirs_of[dz], "s%d" % dz)

    def early_comm(i):
        if i == 2:
            relay_z()
        elif i == 4:
            relay_x(6), relay_x(2)
        elif i == 6:
            relay_x(5), relay_x(3)
        elif i == 7:
            relay_x(4)

    def gather_comm(i):
        if i < 7:
            collect(ORDER[i + 1])
        use(ORDER[i])

    def codes(i, carry):
        for k in range(8):
            @pl.when(i == k)
            def _(k=k):
                early_comm(k)

        slot = lax.rem(i, 3)
        pltpu.make_async_copy(cnt.at[slot], cnt.at[slot], cntsem.at[slot]).wait()

        @pl.when(i < 6)
        def _():
            fetch(i + 2, 0)

        at = pl.multiple_of(i * GRP, GRP)
        sums = []
        for b in range(8):
            rng = pl.ds(pl.multiple_of(at + b * BLK, 16), BLK)
            mass = None
            for kt in range(8):
                v = jnp.concatenate(
                    [cnt[slot, pl.ds(b * vb + kt * 2 + 1 - j, BLK // 2, stride=16), :] for j in range(2)], axis=0
                ).astype(F32)
                mass = v if mass is None else mass + v
                hi, lo = split(v)
                cols = pl.ds(kt * 128, 128)
                qhi[rng, cols] = hi
                qlo[rng, cols] = lo
            sums.append(mass)
        to_rows(jnp.sum(jnp.concatenate(sums, axis=0), axis=1, keepdims=True), select(i, qs), 3)
        rng = pl.ds(at, GRP)
        hi, lo = qhi[rng, :], qlo[rng, :]
        ug[rng, :] = dot(hi, chi[...]) + dot(hi, clo[...]) + dot(lo, chi[...])
        return carry

    def forward(i, carry):
        for k in range(8):
            @pl.when(i == k)
            def _(k=k):
                gather_comm(k)

        group = select(i, qs)
        v = u[pl.ds(pl.multiple_of(group * GRP, 8), GRP), :]
        hi, lo = split(v)
        at = pl.multiple_of(i * GRP, GRP)
        part = None
        for n in range(4):
            cols = pl.ds(n * 256, 256)
            s = dot(hi, cth[:, cols]) + dot(lo, cth[:, cols]) + dot(hi, ctl[:, cols])
            ex = jnp.exp2(s)
            hi_e, lo_e = split(ex)
            ehi[pl.ds(at, GRP), cols] = hi_e
            elo[pl.ds(at, GRP), cols] = lo_e
            two = ex[:, :128] + ex[:, 128:]
            part = two if part is None else part + two
        total = jnp.sum(part, axis=1, keepdims=True)
        hi, lo = split(jnp.transpose(v))
        ut[0:D, pl.ds(at, GRP)] = hi
        ut[D : 2 * D, pl.ds(at, GRP)] = lo
        to_rows(total, group, 0)
        return carry

    lax.fori_loop(0, 8, codes, 0)
    lax.fori_loop(0, 8, forward, 0)

    def small(src, dst, ss, rr, device):
        return pltpu.make_async_remote_copy(
            src_ref=src, dst_ref=dst, send_sem=ss, recv_sem=rr, device_id=device, device_id_type=MESH
        )

    def codes_slab(s):
        cols = pl.ds(s * 256, 256)
        both = dot(ut[...], qhi[:, cols])
        acc = both[:D] + both[D:] + dot(ut[0:D, :], qlo[:, cols])
        pg[cols, :] = jnp.transpose(acc) * (-FIXED_POINT * WEIGHT)

    def forward_grad(i, carry):
        rng = pl.ds(pl.multiple_of(i * GRP, GRP), GRP)
        hi, lo = ehi[rng, :], elo[rng, :]
        ec[rng, :] = dot(hi, chi[...]) + dot(hi, clo[...]) + dot(lo, chi[...])
        return carry

    first = [small(tbuf.at[ranks[k]], t1.at[k], t1s.at[k], t1r.at[k], peers[k]) for k in range(7)]
    for copy in first:
        copy.start()
    codes_slab(0)
    codes_slab(1)
    lax.fori_loop(0, 1, forward_grad, 0)
    for copy in first:
        copy.wait()
    mine = tbuf[g8]
    for k in range(7):
        mine = mine + t1[k]
    t2[7] = mine
    second = [small(t2.at[7], t2.at[k], t2s.at[k], t2r.at[k], zpeers[k]) for k in range(7)]
    for copy in second:
        copy.start()
    codes_slab(2)
    codes_slab(3)
    lax.fori_loop(1, 4, forward_grad, 0)
    for copy in second:
        copy.wait()
    mine = t2[7]
    for k in range(7):
        mine = mine + t2[k]
    t3[g8, 0:3, :] = mine[3:6, :] * (FIXED_POINT * WEIGHT) / mine[0:3, :]
    third = [small(t3.at[g8], t3.at[g8], t3s.at[k], t3r.at[k], peers[k]) for k in range(7)]
    for copy in third:
        copy.start()
    lax.fori_loop(4, 8, forward_grad, 0)
    for k in range(7):
        small(t3.at[ranks[6 - k]], t3.at[ranks[6 - k]], t3s.at[k], t3r.at[k], peers[k]).wait_recv()
    for copy in third:
        copy.wait_send()

    def ypart(s):
        h1, h2 = s * 256, s * 256 + 128

        def ds(at, n):
            return pl.ds(pl.multiple_of(at, 8), n)

        return dict(
            away1=(ds(h1 + (1 - fbit) * 64, 64), ds(h2 + (1 - gbit) * 64, 64)),
            keep1=(ds(h1 + fbit * 64, 64), ds(h2 + gbit * 64, 64)),
            away2=(ds(h1 + fbit * 64 + (1 - gbit) * 32, 32), ds(h2 + gbit * 64 + (1 - fbit) * 32, 32)),
            keep2=(ds(h1 + fbit * 64 + gbit * 32, 32), ds(h2 + gbit * 64 + fbit * 32, 32)),
        )

    yparts = [ypart(s) for s in range(4)]

    def out_copy(s):
        rng = pl.ds(s * 256, 256)
        return pltpu.make_async_copy(pgo.at[rng], pg_out.at[rng], rsem.at[RS["out%d" % s]])

    def ystep(k, s):
        part = yparts[s]
        for h in range(2):
            near, far = (mate_a, mate_b) if h == 0 else (mate_b, mate_a)
            name = "y%d_%d_%d" % (s, k - 1, h)
            prev = "y%d_%d_%d" % (s, k - 2, h)
            if k == 1:
                send(view(pg, (part["away1"][h],)), view(y1, (s, h,)), name, near)
            elif k == 2:
                arrive(y1.at[s, h], prev)
                keep = part["keep1"][h]
                pg[keep, :] = pg[keep, :] + y1[s, h]
                send(view(pg, (part["away2"][h],)), view(y2, (s, h,)), name, far)
            elif k == 3:
                arrive(y2.at[s, h], prev)
                keep = part["keep2"][h]
                pgo[keep, :] = pg[keep, :] + y2[s, h]
                send(view(pgo, (keep,)), view(pgo, (keep,)), name, far)
            elif k == 4:
                arrive(pgo.at[part["away2"][h]], prev)
                send(view(pgo, (part["keep1"][h],)), view(pgo, (part["keep1"][h],)), name, near)
            elif k == 5:
                arrive(pgo.at[part["away1"][h]], prev)
        if k == 5:
            out_copy(s).start()

    def slab(s, carry):
        col = pl.multiple_of(s * 256, 256)

        cols = pl.ds(col, 256)
        both = dot(utw[...], ehi[:, cols])
        acc = both[:D] + both[D:] + dot(utw[0:D, :], elo[:, cols])
        pg[cols, :] = jnp.transpose(acc) + pg[cols, :]
        for k in range(4):
            @pl.when(s == k)
            def _(k=k):
                slab_comm(k)
        return carry

    mine_at = [pl.ds(pl.multiple_of(POS[dz] * GRP + c * HALF, 8), HALF) for dz in range(8)]
    theirs_at = [pl.ds(pl.multiple_of(POS[dz] * GRP + (1 - c) * HALF, 8), HALF) for dz in range(8)]

    def gblk(dz, dx):
        return pl.ds(pl.multiple_of(POS[dz] * GRP + c * HALF + lax.rem(x + dx, XN) * BLK, 8), BLK)

    gb = {(dz, dx): gblk(dz, dx) for dz in range(8) for dx in range(4)}

    def from_sibling(dz):
        arrive(sib.at[dz], "q%d" % dz)
        ug[mine_at[dz], :] = ug[mine_at[dz], :] + sib[dz]

    def sums_out(dz):
        from_sibling(dz)
        if dz in (1, 7):
            send(view(ug, (mine_at[dz],)), view(gnb, (dz // 7,)), "gn%d" % dz, zpeers[dz - 1])
        else:
            for d in (2, 1, 3):
                send(view(ug, (gb[dz, d],)), view(gxb, ((dz - 2) * 3 + d - 1,)), "gx%d_%d" % (dz, d), xpeers[d - 1])

    def sums_onward(dz):
        total = ug[gb[dz, 0], :]
        for d in (1, 2, 3):
            arrive(gxb.at[(dz - 2) * 3 + d - 1], "gx%d_%d" % (dz, d))
            total = total + gxb[(dz - 2) * 3 + d - 1]
        ug[gb[dz, 0], :] = total
        send(view(ug, (gb[dz, 0],)), view(gzb, (dz - 2,)), "gz%d" % dz, zpeers[dz - 1])

    def sums_here():
        from_sibling(0)
        for k, dz in enumerate((1, 7)):
            arrive(gnb.at[k], "gn%d" % dz)
        ug[mine_at[0], :] = ug[mine_at[0], :] + gnb[0] + gnb[1]
        for d in (2, 1, 3):
            send(view(ug, (gb[0, d],)), view(hxb, (d - 1,)), "hx%d" % d, xpeers[d - 1])

    def sums_end():
        total = ug[gb[0, 0], :]
        for d in (1, 2, 3):
            arrive(hxb.at[d - 1], "hx%d" % d)
            total = total + hxb[d - 1]
        for d in (2, 6, 3, 5, 4):
            arrive(gzb.at[d - 2], "gz%d" % d)
            total = total + gzb[d - 2]
        own[...] = total

    def slab_comm(k):
        ystep(1, k)
        if k >= 2:
            ystep(2, k - 2)

    def column(group):
        cols = []
        for k in range(3):
            cols.append(jnp.sum(jnp.where(eye, t3[group, k : k + 1, :], 0.0), axis=1, keepdims=True))
        return jnp.concatenate(cols, axis=0)

    def backward(i, carry):
        rng = pl.ds(pl.multiple_of(select(i, back) * GRP, GRP), GRP)
        w = jnp.broadcast_to(column(select(i, backq)), (GRP, D))
        ug[rng, :] = w * ec[rng, :] - ug[rng, :] * (FIXED_POINT * WEIGHT)
        for k in range(8):
            @pl.when(i == k)
            def _(k=k):
                dz = BACK[k]
                send(view(ug, (theirs_at[dz],)), view(sib, (dz,)), "q%d" % dz, sibling)
        return carry

    def weighted(i, carry):
        group = select(i, qs)
        for k in range(3):
            cols = pl.ds(pl.multiple_of(i * GRP + k * 128, 128), 128)
            v = (ut[0:D, cols].astype(F32) + ut[D : 2 * D, cols].astype(F32)) * t3[group, k : k + 1, :]
            hi, lo = split(v)
            utw[0:D, cols] = hi
            utw[D : 2 * D, cols] = lo
        return carry

    back = [POS[dz] for dz in BACK]
    backq = [zs[dz] for dz in BACK]
    lax.fori_loop(0, 8, backward, 0)
    lax.fori_loop(0, 8, weighted, 0)
    for dz in BACK[:7]:
        sums_out(dz)
    lax.fori_loop(0, 4, slab, 0)

    ystep(2, 2)
    ystep(3, 0)
    sums_here()
    for dz in FAR[:3]:
        sums_onward(dz)
    ystep(2, 3)
    ystep(3, 1)
    for dz in FAR[3:]:
        sums_onward(dz)
    ystep(3, 2)
    ystep(4, 0)
    ystep(3, 3)
    ystep(4, 1)
    ystep(4, 2)
    ystep(5, 0)
    ystep(4, 3)
    sums_end()

    f, norm = load_features()
    unit = f / norm
    grad = own[...]
    inner = jnp.sum(unit * grad, axis=1, keepdims=True)
    out = (grad - unit * inner) / norm
    for j in range(2):
        for kt in range(2):
            piece = out[j * (BLK // 2) : (j + 1) * (BLK // 2), kt * 128 : (kt + 1) * 128]
            fg[pl.ds(kt * 2 + j, BLK // 2, stride=4), :] = piece

    ystep(5, 1)
    ystep(5, 2)
    ystep(5, 3)
    for make in sent:
        make().wait_send()
    for s in range(4):
        out_copy(s).wait()


def hand_over(fg, pg, fg_out, pg_out):
    fg_out[...] = fg[...]
    pg_out[...] = pg[...]


def per_device(features, prototypes, code_counts):
    feat = features.reshape(24, 2, 2, 128).transpose(0, 2, 1, 3).reshape(96, 128)
    counts = code_counts.reshape(1536, 2, 8, 128).transpose(0, 2, 1, 3).reshape(1536 * 16, 128)
    vmem, hbm = pl.BlockSpec(memory_space=pltpu.VMEM), pl.BlockSpec(memory_space=pl.ANY)
    dma = pltpu.SemaphoreType.DMA
    fg, pg = pl.pallas_call(
        kernel,
        out_shape=(jax.ShapeDtypeStruct((96, 128), F32), jax.ShapeDtypeStruct((KL, D), F32)),
        in_specs=[vmem, hbm, hbm],
        out_specs=(vmem, hbm),
        scratch_shapes=[
            pltpu.VMEM((3, 8 * BLK // 2 * 16, 128), jnp.int32),
            pltpu.VMEM((ROWS, D), F32),
            pltpu.VMEM((2 * D, ROWS), BF16),
            pltpu.VMEM((2 * D, ROWS), BF16),
            pltpu.VMEM((ROWS, KL), BF16),
            pltpu.VMEM((ROWS, KL), BF16),
            pltpu.VMEM((ROWS, KL), BF16),
            pltpu.VMEM((ROWS, KL), BF16),
            pltpu.VMEM((ROWS, D), F32),
            pltpu.VMEM((ROWS, D), F32),
            pltpu.VMEM((8, HALF, D), F32),
            pltpu.VMEM((D, KL), BF16),
            pltpu.VMEM((D, KL), BF16),
            pltpu.VMEM((KL, D), BF16),
            pltpu.VMEM((KL, D), BF16),
            pltpu.VMEM((KL, D), F32),
            pltpu.VMEM((KL, D), F32),
            pltpu.VMEM((BLK, D), F32),
            pltpu.VMEM((8, 8, 128), F32),
            pltpu.VMEM((7, 8, 128), F32),
            pltpu.VMEM((8, 8, 128), F32),
            pltpu.VMEM((8, 8, 128), F32),
            pltpu.VMEM((15, BLK, D), F32),
            pltpu.VMEM((2, HALF, D), F32),
            pltpu.VMEM((5, BLK, D), F32),
            pltpu.VMEM((3, BLK, D), F32),
            pltpu.VMEM((4, 2, 64, D), F32),
            pltpu.VMEM((4, 2, 32, D), F32),
            dma((128,)),
            dma((len(RS),)),
            dma((3,)),
            dma((7,)), dma((7,)), dma((7,)), dma((7,)), dma((7,)), dma((7,)),
        ],
        compiler_params=pltpu.CompilerParams(
            collective_id=0, has_side_effects=True, vmem_limit_bytes=60 << 20
        ),
        cost_estimate=pl.CostEstimate(flops=18 * ROWS * KL * D, bytes_accessed=16 << 20, transcendentals=ROWS * KL),
    )(feat, prototypes, counts)
    fg, pg = pl.pallas_call(
        hand_over,
        out_shape=(jax.ShapeDtypeStruct((96, 128), F32), jax.ShapeDtypeStruct((KL, D), F32)),
        in_specs=[vmem, vmem],
        out_specs=(vmem, vmem),
    )(fg, pg)
    features_grad = fg.reshape(24, 2, 2, 128).transpose(0, 2, 1, 3).reshape(24, 2, 256)
    return features_grad, pg


def solution(mesh):
    in_specs = (P(("view", "proto"), None, None), P("proto", None), P("view", None, "proto"))
    out_specs = (P(("view", "proto"), None, None), P("proto", None))
    return jax.shard_map(
        per_device, mesh=mesh, in_specs=in_specs, out_specs=out_specs, check_vma=False
    )
```
